32 devices in a mesh: rep: 2 (over y), exp: 16 (over z, x, core).
Axes of the slice: x: 2, y: 2, z: 4, core: 2. Of those that a mesh axis runs over, the one named last changes fastest.
Arguments:
- tokens: bfloat16 [4096, 3584], P(('rep', 'exp')), may hold values from -6 to 6
- cotangent: bfloat16 [4096, 3584], P(('rep', 'exp')), may hold values from -0.29882812 to 0.29882812
- gates: float32 [4096, 1], P(('rep', 'exp')), may hold values from 0.2 to 1.5
- routes: int32 [4096, 1], P(('rep', 'exp')), may hold values from 0 to 3; in each aligned block of 128 rows (0 to 127, 128 to 255, ...) at most 36 rows name the same one
- w_up: bfloat16 [14336, 1024], P(('exp', 'rep')), may hold values from -0.09375 to 0.09375
- w_down_t: bfloat16 [14336, 1024], P(('exp', 'rep')), may hold values from -0.1875 to 0.1875
Outputs:
- grad_tokens: bfloat16 [4096, 3584], P(('rep', 'exp'))
- grad_gates: float32 [4096, 1], P(('rep', 'exp'))
- grad_up: float32 [14336, 1024], P(('exp', 'rep'))
- grad_down_t: float32 [14336, 1024], P(('exp', 'rep'))
The draws below stay inside these ranges and needn't reach their ends.
Inputs may be any that keep to these rules, and one draw needn't show every extreme that they name: `routes`: each row names one expert (1 = 1). Among the rows of one device no expert is named more than 36 times, and in every draw some expert is named exactly 36 times by the rows of some device.
All inputs are finite; a program needn't handle non-finite values.
Results may differ from the reference program's by a relative error of at most 0.012.
Values may be sent and summed in bfloat16 or wider, within the bound.
A program may use at most 64 MiB of HBM per device.

```python
import math
import jax
import jax.numpy as jnp
import numpy as np
from jax import lax

D = 3584
HID = 1024
SLICES = 4
TOP = 1
TOK_DEV = 128
EXPERTS = 4
CAP = 36
TOKENS = 4096
N_REP = 2
N_EXP = 16


def levels(rng, dims, cuts, smallest, top_value):
    level, own = 1.0, jax.random.fold_in(rng, 6)
    for dim, blocks in cuts:
        steps = jnp.exp(jax.random.uniform(jax.random.fold_in(own, dim), (blocks,), jnp.float32, smallest / len(cuts), top_value / len(cuts)))
        level = level * jnp.repeat(steps, dims[dim] // blocks).reshape([-1 if axis == dim else 1 for axis in range(len(dims))])
    return level


def shared_out(own_key, own, number, rows, count, top, limit, slope):
    order = jax.random.permutation(own_key, count)
    crowded, usual = load_shares(count, rows * top, limit, slope, True), load_shares(count, rows * top, limit, slope, False)
    places = jnp.arange(count)

    def named(tallies, offset_by):
        used = int((tallies > 0).sum())
        fixed = max(1, used // 4)
        passed = fixed + (places - fixed + offset_by * (used - fixed)) % max(1, count - fixed)
        return jnp.zeros((count,), jnp.int32).at[order[jnp.where(places < fixed, places, passed)]].set(jnp.asarray(tallies, jnp.int32))

    tallies = jnp.where(number % 4 == 0, named(crowded, number // 4), named(usual, number - number // 4 - 1))
    mixed = jax.random.permutation(jax.random.fold_in(own, 3), count)
    source_of, receiver = mixed[0:count // 2 * 2:2], mixed[1:count // 2 * 2:2]
    margin = jnp.minimum(tallies[source_of] - 1, limit - tallies[receiver]) // 2
    margin = jnp.where((source_of == order[0]) | (receiver == order[0]) | (tallies[receiver] == 0), 0, jnp.maximum(margin, 0))
    passed = jax.random.randint(jax.random.fold_in(own, 4), (count // 2,), 0, 1 << 20) % (margin + 1)
    tallies = tallies.at[source_of].add(-passed).at[receiver].add(passed)
    members = jnp.searchsorted(jnp.cumsum(tallies), jnp.arange(rows * top), side="right").astype(jnp.int32)
    listing = members.reshape(top, rows).T
    listing = listing[jax.random.permutation(jax.random.fold_in(own, 1), rows)]
    offset_by = jax.random.randint(jax.random.fold_in(own, 2), (rows, 1), 0, top)
    return jnp.take_along_axis(listing, (jnp.arange(top)[None, :] + offset_by) % top, axis=1)


def load_shares(amount, total, limit, slope, full):
    portions = [(1 << 20) // math.isqrt(rank ** slope) + 1 for rank in range(1, amount + 1)]
    largest = limit if full else min(limit, max(-(-total // amount), total * portions[0] // sum(portions)))
    least = 1 if total - largest >= amount - 1 else 0
    given, rest = [largest] + [least] * (amount - 1), total - largest - least * (amount - 1)
    while rest > 0:
        free = [i for i in range(1, amount) if given[i] < largest] or [i for i in range(1, amount) if given[i] < limit]
        mass, left = sum([portions[i] for i in free]), rest
        for i in free:
            more = min(limit - given[i], max(1, left * portions[i] // mass), rest)
            given[i] = given[i] + more
            rest = rest - more
    return np.array(given)


def scatter_about(rng, extent, deviation, bound, split=(), kind=jnp.bfloat16):
    entries = jax.random.normal(rng, extent, jnp.float32) * deviation
    if len(split) > 0:
        entries = levels(rng, extent, split, -0.22, 0.18) * entries
    return jnp.clip(entries, min=-bound, max=bound).astype(kind)


def setup_inputs(seed: int = 0) -> dict:
    keys = jax.random.split(jax.random.key(seed), 7)
    tokens = scatter_about(keys[0], (TOKENS, D), 1.0, 6.0, ((0, 32),))
    cotangent = scatter_about(keys[1], (TOKENS, D), 0.05, 0.29882812, ((0, 32),))
    gates = jnp.clip(0.2 + 1.3 * jax.random.uniform(keys[2], (TOKENS, TOP), jnp.float32) ** levels(keys[2], (TOKENS, TOP), ((0, 32),), -0.2, 0.2), 0.2, 1.5)
    routes_keys = jax.random.split(jax.random.fold_in(keys[3], 1), TOKENS // TOK_DEV)
    routes_turns = jax.random.permutation(jax.random.fold_in(keys[3], 3), TOKENS // TOK_DEV)
    routes = jax.vmap(lambda own, number: shared_out(jax.random.fold_in(keys[3], 2), own, number, TOK_DEV, EXPERTS, TOP, CAP, 2))(routes_keys, routes_turns).reshape((TOKENS, TOP))
    w_up = scatter_about(keys[4], (EXPERTS * D, HID), D ** -0.5, 0.09375, ((0, 32),))
    w_down_t = scatter_about(keys[5], (EXPERTS * D, HID), HID ** -0.5, 0.1875, ((0, 32),))
    return {"tokens": tokens, "cotangent": cotangent, "gates": gates, "routes": routes, "w_up": w_up, "w_down_t": w_down_t}


def slot_numbers(route_rows):
    flat_route = route_rows.reshape(-1)
    onehot = (flat_route[:, None] == jnp.arange(EXPERTS, dtype=jnp.int32)[None, :]).astype(jnp.int32)
    earlier = jnp.cumsum(onehot, axis=0) - onehot
    return jnp.sum(earlier * onehot, axis=1).astype(jnp.int32)


def block_sum(left_side, right_side):
    piece_width = D // SLICES
    total = jnp.zeros((left_side.shape[0], right_side.shape[1]), jnp.float32)
    for slice_number in range(SLICES):
        lower = slice_number * piece_width
        upper = lower + piece_width
        part = jnp.dot(left_side[:, lower:upper], right_side[lower:upper], preferred_element_type=jnp.float32).astype(jnp.bfloat16)
        total = total + lax.optimization_barrier(part).astype(jnp.float32)
    return total


def reference(tokens, cotangent, gates, routes, w_up, w_down_t):
    group_rows = N_EXP * TOK_DEV
    choice_count = group_rows * TOP
    slot_total = N_EXP * CAP
    token_blocks = tokens.reshape(N_REP, group_rows, D)
    cot_blocks = cotangent.reshape(N_REP, group_rows, D)
    gate_blocks = gates.reshape(N_REP, group_rows, TOP)
    route_blocks = routes.reshape(N_REP, group_rows, TOP)

    def replica_step(carry, inputs):
        up_total, down_total = carry
        block_tokens, block_cot, block_gates, block_routes = inputs
        flat_route = block_routes.reshape(-1)
        slot_index = jax.vmap(slot_numbers)(block_routes.reshape(N_EXP, TOK_DEV * TOP)).reshape(-1)
        choice_ids = jnp.arange(choice_count, dtype=jnp.int32)
        source_dev = choice_ids // (TOK_DEV * TOP)
        position = (source_dev * CAP + slot_index).astype(jnp.int32)
        flat_gates = block_gates.reshape(-1)
        repeated = jnp.repeat(block_cot, TOP, axis=0).astype(jnp.float32)
        gate_grad = jnp.zeros((choice_count,), jnp.float32)
        input_grad = jnp.zeros((choice_count, D), jnp.float32)
        up_parts = []
        down_parts = []
        for expert in range(EXPERTS):
            selected = flat_route == expert
            target = jnp.where(selected, position, slot_total).astype(jnp.int32)
            table = jnp.full((slot_total + 1,), -1, dtype=jnp.int32).at[target].set(choice_ids)[:slot_total]
            filled = table >= 0
            chosen = jnp.maximum(table, 0).astype(jnp.int32)
            source_row = (chosen // TOP).astype(jnp.int32)
            inputs_buf = jnp.where(filled[:, None], block_tokens[source_row], jnp.zeros((), block_tokens.dtype))
            weight = flat_gates[chosen]
            grads_buf = jnp.where(filled[:, None], weight[:, None] * block_cot[source_row].astype(jnp.float32), jnp.float32(0.0)).astype(jnp.bfloat16)
            up_matrix = w_up[expert * D:(expert + 1) * D]
            down_matrix = w_down_t[expert * D:(expert + 1) * D]
            activation = block_sum(inputs_buf, up_matrix)
            gating = jax.nn.sigmoid(activation)
            hidden_act = (activation * gating).astype(jnp.bfloat16)
            outputs = jnp.dot(hidden_act, down_matrix.T, preferred_element_type=jnp.float32).astype(jnp.bfloat16)
            hidden_grad = block_sum(grads_buf, down_matrix)
            act_grad = (hidden_grad * gating * (1.0 + activation * (1.0 - gating))).astype(jnp.bfloat16)
            input_part = jnp.dot(act_grad, up_matrix.T, preferred_element_type=jnp.float32).astype(jnp.bfloat16)
            up_parts.append(jnp.dot(inputs_buf.T, act_grad, preferred_element_type=jnp.float32).astype(jnp.bfloat16))
            down_parts.append(jnp.dot(grads_buf.T, hidden_act, preferred_element_type=jnp.float32).astype(jnp.bfloat16))
            lookup = jnp.where(selected, position, 0).astype(jnp.int32)
            picked = outputs[lookup].astype(jnp.float32)
            gate_grad = gate_grad + jnp.where(selected, jnp.sum(repeated * picked, axis=1), jnp.float32(0.0))
            input_grad = input_grad + jnp.where(selected[:, None], input_part[lookup].astype(jnp.float32), jnp.float32(0.0))
        up_total = up_total + jnp.concatenate(up_parts, axis=0).astype(jnp.float32)
        down_total = down_total + jnp.concatenate(down_parts, axis=0).astype(jnp.float32)
        token_grad = jnp.sum(input_grad.reshape(group_rows, TOP, D), axis=1).astype(jnp.bfloat16)
        return (up_total, down_total), (token_grad, gate_grad.reshape(group_rows, TOP))

    start = (jnp.zeros((EXPERTS * D, HID), jnp.float32), jnp.zeros((EXPERTS * D, HID), jnp.float32))
    (grad_up, grad_down_t), (token_grads, gate_grads) = lax.scan(replica_step, start, (token_blocks, cot_blocks, gate_blocks, route_blocks))
    return token_grads.reshape(TOKENS, D), gate_grads.reshape(TOKENS, TOP), grad_up, grad_down_t
```

```python
import jax
import jax.numpy as jnp
from jax import lax
from jax.sharding import PartitionSpec as P

SLICES = 4


def swapped(x, axis, distance):
    return lax.ppermute(x, axis, [(i, i ^ 1 << distance) for i in range(lax.axis_size(axis))])


def contract_last(left_side, right_side):
    return lax.dot_general(
        left_side, right_side, (((1,), (1,)), ((), ())), preferred_element_type=jnp.float32
    )


def contract_first(left_side, right_side):
    return lax.dot_general(
        left_side, right_side, (((0,), (0,)), ((), ())), preferred_element_type=jnp.float32
    )


def shards(tokens, cotangent, gates, routes, w_up, w_down_t):
    tok_dev, top_count = routes.shape
    model_width = tokens.shape[1]
    piece_width = model_width // SLICES
    slice_bits = SLICES.bit_length() - 1
    n_devices = lax.axis_size("exp")
    experts = n_devices // SLICES
    capacity = min(tok_dev, max(2, 9 * tok_dev * top_count // (8 * experts)))
    slot_rows = capacity * n_devices
    exp_index = lax.axis_index("exp")
    up_rows, down_rows = (
        lax.all_gather(w_up, "rep", axis=0, tiled=True),
        lax.all_gather(w_down_t, "rep", axis=0, tiled=True),
    )
    flat_route = routes.reshape(-1)
    choice_count = flat_route.shape[0]
    onehot = (flat_route[:, None] == jnp.arange(experts, dtype=jnp.int32)[None, :]).astype(
        jnp.int32
    )
    earlier = jnp.cumsum(onehot, axis=0) - onehot
    slot_index = jnp.sum(earlier * onehot, axis=1)
    position = slot_index * experts + flat_route
    matches = position[None, :] == jnp.arange(capacity * experts, dtype=jnp.int32)[:, None]
    filled = jnp.any(matches, axis=1)
    chosen = jnp.sum(
        jnp.where(matches, jnp.arange(choice_count, dtype=jnp.int32)[None, :], 0), axis=1
    )
    source_row = chosen // top_count
    weight = gates.reshape(-1)[chosen]
    inputs_buf = jnp.where(filled[:, None], tokens[source_row], jnp.zeros((), tokens.dtype))
    inputs_buf = inputs_buf.reshape(capacity, n_devices, piece_width)
    grads_buf = jnp.where(
        filled[:, None], weight[:, None] * cotangent[source_row].astype(jnp.float32), 0.0
    )
    grads_buf = grads_buf.astype(jnp.bfloat16).reshape(capacity, n_devices, piece_width)
    inputs_in = lax.all_to_all(inputs_buf, "exp", split_axis=1, concat_axis=1, tiled=True)
    x_rows = inputs_in.reshape(slot_rows, piece_width)
    partial_value = jnp.dot(x_rows, up_rows, preferred_element_type=jnp.float32).astype(
        jnp.bfloat16
    )
    stacked = partial_value[None]
    for bit_number in range(slice_bits):
        upper_side = exp_index >> bit_number & 1 == 1
        half_width = stacked.shape[2] // 2
        lower_half = stacked[:, :, :half_width]
        upper_half = stacked[:, :, half_width:]
        kept_half = jnp.where(upper_side, upper_half, lower_half)
        given_half = jnp.where(upper_side, lower_half, upper_half)
        stacked = jnp.concatenate([kept_half, swapped(given_half, "exp", bit_number)], axis=0)
    activation = jnp.sum(stacked.astype(jnp.float32), axis=0)
    gating = jax.nn.sigmoid(activation)
    hidden_act = (activation * gating).astype(jnp.bfloat16)
    for bit_number in reversed(range(slice_bits)):
        upper_side = exp_index >> bit_number & 1 == 1
        partner_cols = swapped(hidden_act, "exp", bit_number)
        hidden_act = jnp.where(
            upper_side,
            jnp.concatenate([partner_cols, hidden_act], axis=1),
            jnp.concatenate([hidden_act, partner_cols], axis=1),
        )
    grads_in = lax.all_to_all(grads_buf, "exp", split_axis=1, concat_axis=1, tiled=True)
    d_rows = grads_in.reshape(slot_rows, piece_width)
    grad_partial = jnp.dot(d_rows, down_rows, preferred_element_type=jnp.float32).astype(
        jnp.bfloat16
    )
    grad_stack = grad_partial[None]
    for bit_number in range(slice_bits):
        upper_side = exp_index >> bit_number & 1 == 1
        half_width = grad_stack.shape[2] // 2
        lower_half = grad_stack[:, :, :half_width]
        upper_half = grad_stack[:, :, half_width:]
        kept_half = jnp.where(upper_side, upper_half, lower_half)
        given_half = jnp.where(upper_side, lower_half, upper_half)
        grad_stack = jnp.concatenate([kept_half, swapped(given_half, "exp", bit_number)], axis=0)
    grad_cols = jnp.sum(grad_stack.astype(jnp.float32), axis=0)
    gate_part = jnp.sum(grad_cols * (activation * gating), axis=1)
    gate_back = lax.all_to_all(
        gate_part.reshape(capacity, n_devices), "exp", split_axis=1, concat_axis=1, tiled=True
    )
    gate_table = jnp.sum(gate_back.reshape(capacity * experts, SLICES), axis=1)
    act_grad = (grad_cols * gating * (1.0 + activation * (1.0 - gating))).astype(jnp.bfloat16)
    for bit_number in reversed(range(slice_bits)):
        upper_side = exp_index >> bit_number & 1 == 1
        partner_cols = swapped(act_grad, "exp", bit_number)
        act_grad = jnp.where(
            upper_side,
            jnp.concatenate([partner_cols, act_grad], axis=1),
            jnp.concatenate([act_grad, partner_cols], axis=1),
        )
    dx_rows = contract_last(act_grad, up_rows).astype(jnp.bfloat16)
    dx_buf = dx_rows.reshape(capacity, n_devices, piece_width)
    up_term = contract_first(x_rows, act_grad)
    down_term = contract_first(d_rows, hidden_act)
    grad_down_t = lax.psum_scatter(
        down_term.astype(jnp.bfloat16), "rep", scatter_dimension=0, tiled=True
    ).astype(jnp.float32)
    grad_up = lax.psum_scatter(
        up_term.astype(jnp.bfloat16), "rep", scatter_dimension=0, tiled=True
    ).astype(jnp.float32)
    dx_back = lax.all_to_all(dx_buf, "exp", split_axis=1, concat_axis=1, tiled=True)
    dx_table = dx_back.reshape(capacity * experts, model_width)
    grad_gates = gate_table[position].reshape(tok_dev, top_count) / gates
    grad_tokens = jnp.sum(
        dx_table[position].astype(jnp.float32).reshape(tok_dev, top_count, model_width), axis=1
    )
    return (grad_tokens.astype(jnp.bfloat16), grad_gates, grad_up, grad_down_t)


def solution(mesh):
    placed = (
        P(("rep", "exp"), None),
        P(("rep", "exp"), None),
        P(("rep", "exp"), None),
        P(("rep", "exp"), None),
        P(("exp", "rep"), None),
        P(("exp", "rep"), None),
    )
    return jax.shard_map(
        shards,
        mesh=mesh,
        in_specs=placed,
        out_specs=(
            P(("rep", "exp"), None),
            P(("rep", "exp"), None),
            P(("exp", "rep"), None),
            P(("exp", "rep"), None),
        ),
        check_vma=False,
    )
```

```python
import functools

import jax
import jax.numpy as jnp
from jax import lax
from jax.experimental import pallas as pl
from jax.experimental.pallas import tpu as pltpu
from jax.sharding import PartitionSpec as P

SLICES = 4
MESH = pl.DeviceIdType.MESH
F32, BF16 = jnp.float32, jnp.bfloat16


def dot(left, right, dims, precision=None):
    return lax.dot_general(
        left, right, ((dims[:1], dims[1:]), ((), ())), preferred_element_type=F32, precision=precision
    )


def tiles(width, step=256):
    return [(start, min(step, width - start)) for start in range(0, width, step)]


def kernel(
    n_rep, planes, capacity, slots,
    tokens, cot, gates, routes, w_up, w_down,
    grad_tokens, gate_sums, weight_sums,
    out_grad, raw, place, weights, packed, rows, part, first, first_in, second_in,
    act, hidden, terms, dx, dx_in, gate_row, gate_in, back, gate_back, gate_mates,
    local_sem, raw_send, raw_recv, place_send, place_recv, weight_send, weight_recv,
    plane_send, plane_recv, a_send, a_recv, b_send, b_recv, c_send, c_recv, d_send, d_recv,
    dx_send, dx_recv, gate_send, gate_recv, term_send, term_recv, back_send, back_recv,
    mate_send, mate_recv,
):
    rep, me = lax.axis_index("rep"), lax.axis_index("exp")
    plane, q = me // SLICES, me % SLICES
    low, high = q % 2, q // 2
    tok_dev, width = tokens.shape[0], raw.shape[3]
    own_rows, hid = w_up.shape
    half, quarter = hid // 2, hid // 4
    items = 2 * planes

    def mate(distance):
        return (rep, plane * SLICES + (q + distance) % SLICES)

    def ahead(distance):
        return (rep, (plane + distance) % planes * SLICES + q)

    def behind(distance):
        return (rep, (plane + planes - distance) % planes * SLICES + q)

    def replica(distance):
        return ((rep + distance) % n_rep, me)

    near = (rep, plane * SLICES + high * 2 + 1 - low)
    far = (rep, plane * SLICES + (1 - high) * 2 + low)

    def copy(source, target, send_sem, recv_sem, device):
        return pltpu.make_async_remote_copy(
            src_ref=source, dst_ref=target, send_sem=send_sem, recv_sem=recv_sem,
            device_id=device, device_id_type=MESH,
        )

    def feature_block(index):
        return pl.ds(pl.multiple_of(index * width, 128), width)

    def weight_rows(index):
        return pl.ds(pl.multiple_of(index * own_rows, 16), own_rows)

    def raw_copy(a, j):
        source = (tokens, out_grad)[a]
        return copy(
            source.at[:, feature_block((q + j) % SLICES)], raw.at[a, q],
            raw_send.at[a, j], raw_recv.at[a, j], mate(j),
        )

    def place_copy(j):
        return copy(place.at[q], place.at[q], place_send.at[j], place_recv.at[j], mate(j))

    def weight_copy(a, d):
        source = (w_up, w_down)[a]
        return copy(
            source, weights.at[a, weight_rows(rep)],
            weight_send.at[a, d], weight_recv.at[a, d], replica(d),
        )

    def plane_copy(a, k):
        return copy(
            packed.at[a, k], rows.at[a, k], plane_send.at[a, k], plane_recv.at[a, k], ahead(k)
        )

    def a_copy(s):
        other = pl.ds(pl.multiple_of((1 - low) * half, 128), half)
        return copy(part.at[s, :, other], first_in.at[s], a_send.at[s], a_recv.at[s], near)

    def b_copy(s):
        other = pl.ds(pl.multiple_of((1 - high) * quarter, 128), quarter)
        return copy(first.at[s, :, other], second_in.at[s], b_send.at[s], b_recv.at[s], far)

    own_quarter = pl.ds(pl.multiple_of(low * half + high * quarter, 128), quarter)
    own_half = pl.ds(pl.multiple_of(low * half, 128), half)

    def c_copy(s):
        block = hidden.at[s, :, own_quarter]
        return copy(block, block, c_send.at[s], c_recv.at[s], far)

    def d_copy(s):
        block = hidden.at[s, :, own_half]
        return copy(block, block, d_send.at[s], d_recv.at[s], near)

    def dx_copy(k):
        return copy(dx.at[k], dx_in.at[k], dx_send.at[k], dx_recv.at[k], behind(k))

    def gate_copy(k):
        return copy(gate_row.at[k], gate_in.at[k], gate_send.at[k], gate_recv.at[k], behind(k))

    def term_copy(a, d):
        return copy(
            terms.at[a, weight_rows((rep + d) % n_rep)], weight_sums.at[a, d],
            term_send.at[a, d], term_recv.at[a, d], replica(d),
        )

    def back_copy(j):
        return copy(
            back.at[j], grad_tokens.at[:, feature_block(q)],
            back_send.at[j], back_recv.at[j], mate(j),
        )

    def mate_copy(j):
        return copy(gate_back.at[j], gate_mates.at[j], mate_send.at[j], mate_recv.at[j], mate(j))

    barrier = pltpu.get_barrier_semaphore()
    peers = [mate(j) for j in range(1, SLICES)] + [replica(d) for d in range(1, n_rep)]
    for device in peers:
        pl.semaphore_signal(barrier, inc=1, device_id=device, device_id_type=MESH)

    @pl.loop(1, planes)
    def _(k):
        pl.semaphore_signal(barrier, inc=1, device_id=ahead(k), device_id_type=MESH)

    pl.semaphore_wait(barrier, len(peers) + planes - 1)

    for j in range(1, SLICES):
        raw_copy(0, j).start()
    for d in range(1, n_rep):
        weight_copy(0, d).start()
    local = [
        pltpu.make_async_copy(tokens.at[:, feature_block(q)], raw.at[0, q], local_sem.at[0]),
        pltpu.make_async_copy(w_up, weights.at[0, weight_rows(rep)], local_sem.at[1]),
        pltpu.make_async_copy(w_down, weights.at[1, weight_rows(rep)], local_sem.at[2]),
    ]
    for c in local:
        c.start()

    route = routes[...]
    count = max(8, planes)
    onehot = (lax.broadcasted_iota(jnp.int32, (count, tok_dev), 0) == route).astype(F32)
    before = (
        lax.broadcasted_iota(jnp.int32, (tok_dev, tok_dev), 0)
        < lax.broadcasted_iota(jnp.int32, (tok_dev, tok_dev), 1)
    ).astype(F32)
    slot = jnp.sum(onehot * dot(onehot, before, (1, 0)), axis=0, keepdims=True)
    position = (route * slots + q * capacity).astype(F32) + slot
    place[q] = jnp.broadcast_to(position, (8, tok_dev))
    for j in range(1, SLICES):
        place_copy(j).start()

    gate = gates[...]
    for m in range(SLICES):
        block = slice(m * width, (m + 1) * width)
        out_grad[:, block] = (gate * cot[:, block].astype(F32)).astype(BF16)
    for j in range(1, SLICES):
        raw_copy(1, j).start()
    for d in range(1, n_rep):
        weight_copy(1, d).start()
    local_grad = pltpu.make_async_copy(
        out_grad.at[:, feature_block(q)], raw.at[1, q], local_sem.at[3]
    )
    local_grad.start()
    gate_row[...] = jnp.zeros_like(gate_row)

    for j in range(1, SLICES):
        place_copy(j).wait_recv()
    places = jnp.concatenate([place[m, 0:1, :] for m in range(SLICES)], axis=1)

    def chosen(expert, positions, kind):
        number = lax.broadcasted_iota(jnp.int32, (slots, positions.shape[1]), 0) + expert * slots
        return jnp.where(number.astype(F32) == positions, 1.0, 0.0).astype(kind)

    def pack(a, k, target):
        matrix = chosen((plane + k) % planes, places, BF16)
        for start, size in tiles(width):
            source = raw[a, :, :, start : start + size].reshape(SLICES * tok_dev, size)
            target[a, k, :, start : start + size] = dot(matrix, source, (1, 0)).astype(BF16)

    for a in range(2):
        for j in range(1, SLICES):
            sender = (q + SLICES - j) % SLICES
            copy(
                raw.at[a, sender], raw.at[a, sender], raw_send.at[a, j], raw_recv.at[a, j], mate(j)
            ).wait_recv()
        (local[0], local_grad)[a].wait()

        @pl.loop(1, planes)
        def _(k):
            pack(a, k, packed)
            plane_copy(a, k).start()

        pack(a, 0, rows)
    local[1].wait()
    local[2].wait()

    def weight_term(a):
        @pl.loop(0, width // 128)
        def _(i):
            features = pl.ds(pl.multiple_of(i * 128, 128), 128)
            left = rows[a, :, :, features].reshape(planes * slots, 128)
            for start, size in tiles(hid, 512):
                right = hidden[(1 - a) * planes : (2 - a) * planes, :, start : start + size]
                right = right.reshape(planes * slots, size)
                terms[a, features, start : start + size] = dot(left, right, (0, 0)).astype(BF16)

        for d in range(1, n_rep):
            term_copy(a, d).start()
        weight_sums[a, 0] = terms[a, weight_rows(rep), :]

    @pl.loop(0, items + 4)
    def _(s):
        @pl.when(s < items)
        def _():
            a, k = s // planes, s % planes

            @pl.when(k == 0)
            def _():
                for d in range(1, n_rep):
                    landed = weights.at[a, weight_rows((rep + n_rep - d) % n_rep)]
                    copy(
                        landed, landed, weight_send.at[a, d], weight_recv.at[a, d], replica(d)
                    ).wait_recv()

            @pl.when(k > 0)
            def _():
                plane_copy(a, k).wait_recv()

            left = rows[a, k]
            for start, size in tiles(hid):
                part[s, :, start : start + size] = dot(
                    left, weights[a, :, start : start + size], (1, 0)
                ).astype(BF16)
            a_copy(s).start()

        @pl.when(s >= 4)
        def _():
            t = s - 4
            landed = hidden.at[t, :, pl.ds(pl.multiple_of((1 - low) * half, 128), half)]
            copy(landed, landed, d_send.at[t], d_recv.at[t], near).wait_recv()

            @pl.when(t >= planes)
            def _():
                k = t - planes
                left = hidden[t]
                for start, size in tiles(width):
                    dx[k, :, start : start + size] = dot(
                        left, weights[0, start : start + size, :], (1, 1)
                    ).astype(BF16)

                @pl.when(k > 0)
                def _():
                    gate_copy(k).start()
                    dx_copy(k).start()

        @pl.when((s >= 3) & (s < items + 3))
        def _():
            t = s - 3
            landed = hidden.at[
                t, :, pl.ds(pl.multiple_of(low * half + (1 - high) * quarter, 128), quarter)
            ]
            copy(landed, landed, c_send.at[t], c_recv.at[t], far).wait_recv()
            d_copy(t).start()

        @pl.when((s >= 2) & (s < items + 2))
        def _():
            t = s - 2
            b_copy(t).wait_recv()
            mine = pl.ds(pl.multiple_of(high * quarter, 128), quarter)
            total = first[t, :, mine].astype(F32) + second_in[t].astype(F32)

            @pl.when(t < planes)
            def _():
                act[t] = total
                hidden[t, :, own_quarter] = (total * jax.nn.sigmoid(total)).astype(BF16)

            @pl.when(t >= planes)
            def _():
                k = t - planes
                value = act[k]
                gating = jax.nn.sigmoid(value)
                hidden[t, :, own_quarter] = (
                    total * gating * (1.0 + value * (1.0 - gating))
                ).astype(BF16)
                gate_row[k, :, 0:slots] = dot(
                    jnp.ones((8, quarter), F32), total * (value * gating), (1, 1),
                    lax.Precision.HIGHEST,
                )

            c_copy(t).start()

        @pl.when((s >= 1) & (s < items + 1))
        def _():
            t = s - 1
            a_copy(t).wait_recv()
            first[t] = (part[t, :, own_half].astype(F32) + first_in[t].astype(F32)).astype(BF16)
            b_copy(t).start()

        @pl.when(s == items)
        def _():
            weight_term(1)

    weight_term(0)

    @pl.loop(1, planes)
    def _(k):
        gate_copy(k).wait_recv()
        dx_copy(k).wait_recv()

    for j in (2, 1, 3, 0):
        positions = place[(q + j) % SLICES][0:1, :]
        blocks = [chosen((plane + k) % planes, positions, BF16) for k in range(planes)]
        matrix = jnp.concatenate(blocks, axis=0)
        for start, size in tiles(width):
            landed = jnp.concatenate(
                [dx[0, :, start : start + size]]
                + [dx_in[k, :, start : start + size] for k in range(1, planes)],
                axis=0,
            )
            back[j, :, start : start + size] = dot(matrix, landed, (0, 0)).astype(BF16)
        sums = jnp.zeros((8, tok_dev), F32)
        for k in range(planes):
            source = gate_row if k == 0 else gate_in
            sums += dot(
                source[k, :, 0:slots], blocks[k].astype(F32), (1, 0), lax.Precision.HIGHEST
            )
        gate_back[j] = sums
        if j > 0:
            back_copy(j).start()
            mate_copy(j).start()
    last = pltpu.make_async_copy(
        back.at[0], grad_tokens.at[:, feature_block(q)], local_sem.at[0]
    )
    last.start()
    total = gate_back[0]
    for j in range(1, SLICES):
        mate_copy(j).wait_recv()
        total += gate_mates[j]
    gate_sums[...] = total
    last.wait()
    for j in range(1, SLICES):
        landed = grad_tokens.at[:, feature_block((q + SLICES - j) % SLICES)]
        copy(landed, landed, back_send.at[j], back_recv.at[j], mate(j)).wait_recv()
    for a in range(2):
        for d in range(1, n_rep):
            term_copy(a, d).wait_recv()
            term_copy(a, d).wait_send()
            weight_copy(a, d).wait_send()
        for j in range(1, SLICES):
            raw_copy(a, j).wait_send()

        @pl.loop(1, planes)
        def _(k):
            plane_copy(a, k).wait_send()

    for j in range(1, SLICES):
        place_copy(j).wait_send()
        back_copy(j).wait_send()
        mate_copy(j).wait_send()

    @pl.loop(1, planes)
    def _(k):
        dx_copy(k).wait_send()
        gate_copy(k).wait_send()

    @pl.loop(0, items)
    def _(s):
        a_copy(s).wait_send()
        b_copy(s).wait_send()
        c_copy(s).wait_send()
        d_copy(s).wait_send()


def shards(tokens, cotangent, gates, routes, w_up, w_down_t):
    tok_dev, top_count = routes.shape
    model_width = tokens.shape[1]
    width = model_width // SLICES
    n_rep, n_exp = lax.axis_size("rep"), lax.axis_size("exp")
    planes = n_exp // SLICES
    capacity = min(tok_dev, max(2, 9 * tok_dev * top_count // (8 * planes)))
    slots = -(-SLICES * capacity // 16) * 16
    lanes = -(-slots // 128) * 128
    own_rows, hid = w_up.shape
    items = 2 * planes
    dma = pltpu.SemaphoreType.DMA
    vmem = pl.BlockSpec(memory_space=pltpu.VMEM)
    pairs = []
    for shape in (
        (2, SLICES), (SLICES,), (2, n_rep), (2, planes), (items,), (items,), (items,), (items,),
        (planes,), (planes,), (2, n_rep), (SLICES,), (SLICES,),
    ):
        pairs += [dma(shape), dma(shape)]
    grad_tokens, gate_sums, weight_sums = pl.pallas_call(
        functools.partial(kernel, n_rep, planes, capacity, slots),
        out_shape=(
            jax.ShapeDtypeStruct((tok_dev, model_width), BF16),
            jax.ShapeDtypeStruct((8, tok_dev), F32),
            jax.ShapeDtypeStruct((2, n_rep, own_rows, hid), BF16),
        ),
        in_specs=[vmem] * 6,
        out_specs=(vmem, vmem, vmem),
        scratch_shapes=[
            pltpu.VMEM((tok_dev, model_width), BF16),
            pltpu.VMEM((2, SLICES, tok_dev, width), BF16),
            pltpu.VMEM((SLICES, 8, tok_dev), F32),
            pltpu.VMEM((2, width, hid), BF16),
            pltpu.VMEM((2, planes, slots, width), BF16),
            pltpu.VMEM((2, planes, slots, width), BF16),
            pltpu.VMEM((items, slots, hid), BF16),
            pltpu.VMEM((items, slots, hid // 2), BF16),
            pltpu.VMEM((items, slots, hid // 2), BF16),
            pltpu.VMEM((items, slots, hid // 4), BF16),
            pltpu.VMEM((planes, slots, hid // 4), F32),
            pltpu.VMEM((items, slots, hid), BF16),
            pltpu.VMEM((2, width, hid), BF16),
            pltpu.VMEM((planes, slots, width), BF16),
            pltpu.VMEM((planes, slots, width), BF16),
            pltpu.VMEM((planes, 8, lanes), F32),
            pltpu.VMEM((planes, 8, lanes), F32),
            pltpu.VMEM((SLICES, tok_dev, width), BF16),
            pltpu.VMEM((SLICES, 8, tok_dev), F32),
            pltpu.VMEM((SLICES, 8, tok_dev), F32),
            dma((4,)),
            *pairs,
        ],
        compiler_params=pltpu.CompilerParams(
            collective_id=0, has_side_effects=True, vmem_limit_bytes=56 * 1024 * 1024
        ),
        cost_estimate=pl.CostEstimate(
            flops=12 * planes * slots * width * hid, bytes_accessed=8 * 1024 * 1024, transcendentals=0
        ),
    )(tokens, cotangent, gates, routes.reshape(1, tok_dev), w_up, w_down_t)
    grads = jnp.sum(weight_sums.astype(F32), axis=1)
    grad_gates = gate_sums[0].reshape(tok_dev, top_count) / gates
    return grad_tokens, grad_gates, grads[0], grads[1]


def solution(mesh):
    split = P(("rep", "exp"), None)
    weight_split = P(("exp", "rep"), None)
    return jax.shard_map(
        shards,
        mesh=mesh,
        in_specs=(split, split, split, split, weight_split, weight_split),
        out_specs=(split, split, weight_split, weight_split),
        check_vma=False,
    )
```

```python
import functools

import jax
import jax.numpy as jnp
from jax import lax
from jax.experimental import pallas as pl
from jax.experimental.pallas import tpu as pltpu
from jax.sharding import PartitionSpec as P

SLICES = 4
MESH = pl.DeviceIdType.MESH
F32, BF16 = jnp.float32, jnp.bfloat16


def dot(left, right, dims, precision=None):
    return lax.dot_general(
        left, right, ((dims[:1], dims[1:]), ((), ())), preferred_element_type=F32, precision=precision
    )


def tiles(width, step=256):
    return [(start, min(step, width - start)) for start in range(0, width, step)]


def kernel(
    n_rep, planes, capacity, slots,
    tokens, cot, gates, routes, w_up, w_down,
    grad_tokens, gate_sums, up_sums, down_sums,
    cot_block, out_grad, raw, place, weights, packed, rows, part, first, first_in, second_in,
    act, hidden, terms, dx, dx_in, gate_row, gate_in, back, gate_back, gate_mates,
    local_sem, raw_send, raw_recv, place_send, place_recv, weight_send, weight_recv,
    plane_send, plane_recv, a_send, a_recv, b_send, b_recv, c_send, c_recv, d_send, d_recv,
    dx_send, dx_recv, gate_send, gate_recv, term_send, term_recv, back_send, back_recv,
    mate_send, mate_recv,
):
    rep, me = lax.axis_index("rep"), lax.axis_index("exp")
    plane, q = me // SLICES, me % SLICES
    low, high = q % 2, q // 2
    tok_dev, width = raw.shape[2], raw.shape[3]
    own_rows, hid = w_up.shape
    half, quarter = hid // 2, hid // 4
    items = 2 * planes
    hops = planes - 1
    last_slot = planes + 4 * hops

    def mate(distance):
        return (rep, plane * SLICES + (q + distance) % SLICES)

    def ahead(distance):
        return (rep, (plane + distance) % planes * SLICES + q)

    def behind(distance):
        return (rep, (plane + planes - distance) % planes * SLICES + q)

    def replica(distance):
        return ((rep + distance) % n_rep, me)

    near = (rep, plane * SLICES + high * 2 + 1 - low)
    far = (rep, plane * SLICES + (1 - high) * 2 + low)

    def copy(source, target, send_sem, recv_sem, device):
        return pltpu.make_async_remote_copy(
            src_ref=source, dst_ref=target, send_sem=send_sem, recv_sem=recv_sem,
            device_id=device, device_id_type=MESH,
        )

    def feature_block(index):
        return pl.ds(pl.multiple_of(index * width, 128), width)

    def weight_rows(index):
        return pl.ds(pl.multiple_of(index * own_rows, 16), own_rows)

    def raw_copy(a, j):
        source = (tokens, out_grad)[a]
        return copy(
            source.at[:, feature_block((q + j) % SLICES)], raw.at[a, q],
            raw_send.at[a, j], raw_recv.at[a, j], mate(j),
        )

    def place_copy(j):
        return copy(place.at[q], place.at[q], place_send.at[j], place_recv.at[j], mate(j))

    def weight_copy(a, d):
        source = (w_up, w_down)[a]
        return copy(
            source, weights.at[a, weight_rows(rep)],
            weight_send.at[a, d], weight_recv.at[a, d], replica(d),
        )

    def plane_copy(a, k):
        return copy(
            packed.at[a, k], rows.at[a, k], plane_send.at[a, k], plane_recv.at[a, k], ahead(k)
        )

    def a_copy(s):
        other = pl.ds(pl.multiple_of((1 - low) * half, 128), half)
        return copy(part.at[s, :, other], first_in.at[s], a_send.at[s], a_recv.at[s], near)

    def b_copy(s):
        other = pl.ds(pl.multiple_of((1 - high) * quarter, 128), quarter)
        return copy(first.at[s, :, other], second_in.at[s], b_send.at[s], b_recv.at[s], far)

    own_quarter = pl.ds(pl.multiple_of(low * half + high * quarter, 128), quarter)
    own_half = pl.ds(pl.multiple_of(low * half, 128), half)

    def c_copy(s):
        block = hidden.at[s, :, own_quarter]
        return copy(block, block, c_send.at[s], c_recv.at[s], far)

    def d_copy(s):
        block = hidden.at[s, :, own_half]
        return copy(block, block, d_send.at[s], d_recv.at[s], near)

    def dx_copy(k):
        return copy(dx.at[k], dx_in.at[k], dx_send.at[k], dx_recv.at[k], behind(k))

    def gate_copy(k):
        return copy(gate_row.at[k], gate_in.at[k], gate_send.at[k], gate_recv.at[k], behind(k))

    def term_copy(a, d):
        return copy(
            terms.at[a, weight_rows((rep + d) % n_rep)], (up_sums, down_sums)[a].at[d],
            term_send.at[a, d], term_recv.at[a, d], replica(d),
        )

    def back_copy(j):
        return copy(
            back.at[j], grad_tokens.at[:, feature_block(q)],
            back_send.at[j], back_recv.at[j], mate(j),
        )

    def mate_copy(j):
        return copy(gate_back.at[j], gate_mates.at[j], mate_send.at[j], mate_recv.at[j], mate(j))

    def term_local(a):
        return pltpu.make_async_copy(
            terms.at[a, weight_rows(rep)], (up_sums, down_sums)[a].at[0], local_sem.at[a]
        )

    cot_local = pltpu.make_async_copy(cot, cot_block, local_sem.at[4])
    cot_local.start()
    barrier = pltpu.get_barrier_semaphore()
    peers = [mate(j) for j in range(1, SLICES)] + [replica(d) for d in range(1, n_rep)]
    for device in peers:
        pl.semaphore_signal(barrier, inc=1, device_id=device, device_id_type=MESH)

    @pl.loop(1, planes)
    def _(k):
        pl.semaphore_signal(barrier, inc=1, device_id=ahead(k), device_id_type=MESH)

    pl.semaphore_wait(barrier, len(peers) + planes - 1)

    for j in range(1, SLICES):
        raw_copy(0, j).start()
    for d in range(1, n_rep):
        weight_copy(0, d).start()
    local = [
        pltpu.make_async_copy(tokens.at[:, feature_block(q)], raw.at[0, q], local_sem.at[0]),
        pltpu.make_async_copy(w_up, weights.at[0, weight_rows(rep)], local_sem.at[1]),
        pltpu.make_async_copy(w_down, weights.at[1, weight_rows(rep)], local_sem.at[2]),
    ]
    for c in local:
        c.start()

    route = routes[...]
    count = max(8, planes)
    onehot = (lax.broadcasted_iota(jnp.int32, (count, tok_dev), 0) == route).astype(F32)
    before = (
        lax.broadcasted_iota(jnp.int32, (tok_dev, tok_dev), 0)
        < lax.broadcasted_iota(jnp.int32, (tok_dev, tok_dev), 1)
    ).astype(F32)
    slot = jnp.sum(onehot * dot(onehot, before, (1, 0)), axis=0, keepdims=True)
    position = (route * slots + q * capacity).astype(F32) + slot
    place[q] = jnp.broadcast_to(position, (8, tok_dev))
    for j in range(1, SLICES):
        place_copy(j).start()

    square = lax.broadcasted_iota(jnp.int32, (tok_dev, tok_dev), 0) == lax.broadcasted_iota(
        jnp.int32, (tok_dev, tok_dev), 1
    )
    gate = jnp.sum(jnp.where(square, gates[...], 0.0), axis=1, keepdims=True)
    cot_local.wait()
    for m in range(SLICES):
        block = slice(m * width, (m + 1) * width)
        out_grad[:, block] = (gate * cot_block[:, block].astype(F32)).astype(BF16)
    local_grad = pltpu.make_async_copy(
        out_grad.at[:, feature_block(q)], raw.at[1, q], local_sem.at[3]
    )
    local_grad.start()
    gate_row[...] = jnp.zeros_like(gate_row)

    for j in range(1, SLICES):
        place_copy(j).wait_recv()
    places = jnp.concatenate([place[m, 0:1, :] for m in range(SLICES)], axis=1)

    def chosen(expert, positions, kind):
        number = lax.broadcasted_iota(jnp.int32, (slots, positions.shape[1]), 0) + expert * slots
        return jnp.where(number.astype(F32) == positions, 1.0, 0.0).astype(kind)

    def pack(a, k, target):
        matrix = chosen((plane + k) % planes, places, BF16)
        for start, size in tiles(width):
            source = raw[a, :, :, start : start + size].reshape(SLICES * tok_dev, size)
            target[a, k, :, start : start + size] = dot(matrix, source, (1, 0)).astype(BF16)

    for a in range(2):
        for j in range(1, SLICES):
            sender = (q + SLICES - j) % SLICES
            copy(
                raw.at[a, sender], raw.at[a, sender], raw_send.at[a, j], raw_recv.at[a, j], mate(j)
            ).wait_recv()
        (local[0], local_grad)[a].wait()
        if a == 0:
            for j in range(1, SLICES):
                raw_copy(1, j).start()

        @pl.loop(1, planes)
        def _(k):
            pack(a, k, packed)
            if a == 0:
                @pl.when(k < 3)
                def _():
                    plane_copy(0, k).start()

        pack(a, 0, rows)
    local[1].wait()
    local[2].wait()

    def weight_term(a):
        @pl.loop(0, width // 128)
        def _(i):
            features = pl.ds(pl.multiple_of(i * 128, 128), 128)
            left = rows[a, :, :, features].reshape(planes * slots, 128)
            for start, size in tiles(hid, 512):
                right = hidden[(1 - a) * planes : (2 - a) * planes, :, start : start + size]
                right = right.reshape(planes * slots, size)
                terms[a, features, start : start + size] = dot(left, right, (0, 0)).astype(BF16)

        for d in range(1, n_rep):
            term_copy(a, d).start()
        term_local(a).start()

    @pl.loop(0, last_slot + 5)
    def _(s):
        def stage(lag):
            slot = s - lag
            extra = slot - planes
            item = jnp.where(extra > 0, planes + extra // 4, slot)
            return item, (slot >= 0) & (slot <= last_slot) & ((extra <= 0) | (extra % 4 == 0))

        e_item, e_here = stage(4)

        @pl.when(e_here)
        def _():
            t = e_item
            landed = hidden.at[t, :, pl.ds(pl.multiple_of((1 - low) * half, 128), half)]
            copy(landed, landed, d_send.at[t], d_recv.at[t], near).wait_recv()

            @pl.when(t >= planes)
            def _():
                k = t - planes
                left = hidden[t]
                for start, size in tiles(width):
                    dx[k, :, start : start + size] = dot(
                        left, weights[0, start : start + size, :], (1, 1)
                    ).astype(BF16)

                @pl.when(k > 0)
                def _():
                    gate_copy(k).start()
                    dx_copy(k).start()

        d_item, d_here = stage(3)

        @pl.when(d_here)
        def _():
            t = d_item
            landed = hidden.at[
                t, :, pl.ds(pl.multiple_of(low * half + (1 - high) * quarter, 128), quarter)
            ]
            copy(landed, landed, c_send.at[t], c_recv.at[t], far).wait_recv()
            d_copy(t).start()

        c_item, c_here = stage(2)

        @pl.when(c_here)
        def _():
            t = c_item
            b_copy(t).wait_recv()
            mine = pl.ds(pl.multiple_of(high * quarter, 128), quarter)
            total = first[t, :, mine].astype(F32) + second_in[t].astype(F32)

            @pl.when(t < planes)
            def _():
                act[t] = total
                hidden[t, :, own_quarter] = (total * jax.nn.sigmoid(total)).astype(BF16)

            @pl.when(t >= planes)
            def _():
                k = t - planes
                value = act[k]
                gating = jax.nn.sigmoid(value)
                hidden[t, :, own_quarter] = (
                    total * gating * (1.0 + value * (1.0 - gating))
                ).astype(BF16)
                gate_row[k, :, 0:slots] = dot(
                    jnp.ones((8, quarter), F32), total * (value * gating), (1, 1),
                    lax.Precision.HIGHEST,
                )

            c_copy(t).start()

        b_item, b_here = stage(1)

        @pl.when(b_here)
        def _():
            t = b_item
            a_copy(t).wait_recv()
            first[t] = (part[t, :, own_half].astype(F32) + first_in[t].astype(F32)).astype(BF16)
            b_copy(t).start()

        i, here = stage(0)

        @pl.when(here)
        def _():
            a, k = i // planes, i % planes

            @pl.when(k == 0)
            def _():
                for d in range(1, n_rep):
                    landed = weights.at[a, weight_rows((rep + n_rep - d) % n_rep)]
                    copy(
                        landed, landed, weight_send.at[a, d], weight_recv.at[a, d], replica(d)
                    ).wait_recv()

                @pl.when(a == 0)
                def _():
                    for d in range(1, n_rep):
                        weight_copy(1, d).start()

            @pl.when(k > 0)
            def _():
                plane_copy(a, k).wait_recv()
                later = a * hops + k + 1

                @pl.when(later < 2 * hops)
                def _():
                    plane_copy(later // hops, later % hops + 1).start()

            left = rows[a, k]
            for start, size in tiles(hid):
                part[i, :, start : start + size] = dot(
                    left, weights[a, :, start : start + size], (1, 0)
                ).astype(BF16)
            a_copy(i).start()

        @pl.when(s == last_slot + 1)
        def _():
            weight_term(1)

    weight_term(0)

    @pl.loop(1, planes)
    def _(k):
        gate_copy(k).wait_recv()
        dx_copy(k).wait_recv()

    for j in (2, 1, 3, 0):
        positions = place[(q + j) % SLICES][0:1, :]
        blocks = [chosen((plane + k) % planes, positions, BF16) for k in range(planes)]
        matrix = jnp.concatenate(blocks, axis=0)
        for start, size in tiles(width):
            landed = jnp.concatenate(
                [dx[0, :, start : start + size]]
                + [dx_in[k, :, start : start + size] for k in range(1, planes)],
                axis=0,
            )
            back[j, :, start : start + size] = dot(matrix, landed, (0, 0)).astype(BF16)
        sums = jnp.zeros((8, tok_dev), F32)
        for k in range(planes):
            source = gate_row if k == 0 else gate_in
            sums += dot(
                source[k, :, 0:slots], blocks[k].astype(F32), (1, 0), lax.Precision.HIGHEST
            )
        gate_back[j] = sums
        if j > 0:
            back_copy(j).start()
            mate_copy(j).start()
    last = pltpu.make_async_copy(
        back.at[0], grad_tokens.at[:, feature_block(q)], local_sem.at[2]
    )
    last.start()
    total = gate_back[0]
    for j in range(1, SLICES):
        mate_copy(j).wait_recv()
        total += gate_mates[j]
    gate_sums[...] = total[0:1] / gates[...]
    last.wait()
    for j in range(1, SLICES):
        landed = grad_tokens.at[:, feature_block((q + SLICES - j) % SLICES)]
        copy(landed, landed, back_send.at[j], back_recv.at[j], mate(j)).wait_recv()
    for a in range(2):
        term_local(a).wait()
        for d in range(1, n_rep):
            term_copy(a, d).wait_recv()
            term_copy(a, d).wait_send()
            weight_copy(a, d).wait_send()
        for j in range(1, SLICES):
            raw_copy(a, j).wait_send()

        @pl.loop(1, planes)
        def _(k):
            plane_copy(a, k).wait_send()

    for j in range(1, SLICES):
        place_copy(j).wait_send()
        back_copy(j).wait_send()
        mate_copy(j).wait_send()

    @pl.loop(1, planes)
    def _(k):
        dx_copy(k).wait_send()
        gate_copy(k).wait_send()

    @pl.loop(0, items)
    def _(s):
        a_copy(s).wait_send()
        b_copy(s).wait_send()
        c_copy(s).wait_send()
        d_copy(s).wait_send()


def shards(tokens, cotangent, gates, routes, w_up, w_down_t):
    tok_dev, top_count = routes.shape
    model_width = tokens.shape[1]
    width = model_width // SLICES
    n_rep, n_exp = lax.axis_size("rep"), lax.axis_size("exp")
    planes = n_exp // SLICES
    capacity = min(tok_dev, max(2, 9 * tok_dev * top_count // (8 * planes)))
    slots = -(-SLICES * capacity // 16) * 16
    lanes = -(-slots // 128) * 128
    own_rows, hid = w_up.shape
    items = 2 * planes
    dma = pltpu.SemaphoreType.DMA
    vmem = pl.BlockSpec(memory_space=pltpu.VMEM)
    hbm = pl.BlockSpec(memory_space=pl.ANY)
    pairs = []
    for shape in (
        (2, SLICES), (SLICES,), (2, n_rep), (2, planes), (items,), (items,), (items,), (items,),
        (planes,), (planes,), (2, n_rep), (SLICES,), (SLICES,),
    ):
        pairs += [dma(shape), dma(shape)]
    grad_tokens, gate_sums, up_sums, down_sums = pl.pallas_call(
        functools.partial(kernel, n_rep, planes, capacity, slots),
        out_shape=(
            jax.ShapeDtypeStruct((tok_dev, model_width), BF16),
            jax.ShapeDtypeStruct((1, tok_dev), F32),
            jax.ShapeDtypeStruct((n_rep, own_rows, hid), BF16),
            jax.ShapeDtypeStruct((n_rep, own_rows, hid), BF16),
        ),
        in_specs=[hbm, hbm, vmem, vmem, hbm, hbm],
        out_specs=(hbm, vmem, hbm, hbm),
        scratch_shapes=[
            pltpu.VMEM((tok_dev, model_width), BF16),
            pltpu.VMEM((tok_dev, model_width), BF16),
            pltpu.VMEM((2, SLICES, tok_dev, width), BF16),
            pltpu.VMEM((SLICES, 8, tok_dev), F32),
            pltpu.VMEM((2, width, hid), BF16),
            pltpu.VMEM((2, planes, slots, width), BF16),
            pltpu.VMEM((2, planes, slots, width), BF16),
            pltpu.VMEM((items, slots, hid), BF16),
            pltpu.VMEM((items, slots, hid // 2), BF16),
            pltpu.VMEM((items, slots, hid // 2), BF16),
            pltpu.VMEM((items, slots, hid // 4), BF16),
            pltpu.VMEM((planes, slots, hid // 4), F32),
            pltpu.VMEM((items, slots, hid), BF16),
            pltpu.VMEM((2, width, hid), BF16),
            pltpu.VMEM((planes, slots, width), BF16),
            pltpu.VMEM((planes, slots, width), BF16),
            pltpu.VMEM((planes, 8, lanes), F32),
            pltpu.VMEM((planes, 8, lanes), F32),
            pltpu.VMEM((SLICES, tok_dev, width), BF16),
            pltpu.VMEM((SLICES, 8, tok_dev), F32),
            pltpu.VMEM((SLICES, 8, tok_dev), F32),
            dma((5,)),
            *pairs,
        ],
        compiler_params=pltpu.CompilerParams(
            collective_id=0, has_side_effects=True, vmem_limit_bytes=56 * 1024 * 1024
        ),
        cost_estimate=pl.CostEstimate(
            flops=12 * planes * slots * width * hid, bytes_accessed=8 * 1024 * 1024, transcendentals=0
        ),
    )(tokens, cotangent, gates.reshape(1, tok_dev), routes.reshape(1, tok_dev), w_up, w_down_t)
    grad_up = jnp.sum(up_sums.astype(F32), axis=0)
    grad_down_t = jnp.sum(down_sums.astype(F32), axis=0)
    return grad_tokens, gate_sums.reshape(tok_dev, top_count), grad_up, grad_down_t


def solution(mesh):
    split = P(("rep", "exp"), None)
    weight_split = P(("exp", "rep"), None)
    return jax.shard_map(
        shards,
        mesh=mesh,
        in_specs=(split, split, split, split, weight_split, weight_split),
        out_specs=(split, split, weight_split, weight_split),
        check_vma=False,
    )
```

```python
import functools

import jax
import jax.numpy as jnp
from jax import lax
from jax.experimental import pallas as pl
from jax.experimental.pallas import tpu as pltpu
from jax.sharding import PartitionSpec as P

SLICES = 4
MESH = pl.DeviceIdType.MESH
F32, BF16 = jnp.float32, jnp.bfloat16


def dot(left, right, dims, precision=None):
    return lax.dot_general(
        left, right, ((dims[:1], dims[1:]), ((), ())), preferred_element_type=F32, precision=precision
    )


def tiles(width, step=256):
    return [(start, min(step, width - start)) for start in range(0, width, step)]


def kernel(
    n_rep, planes, capacity, slots,
    tokens, cot, gates, routes, w_up, w_down,
    grad_tokens, gate_sums, up_sums, down_sums,
    cot_block, out_grad, raw, place, weights, packed, rows, part, first, first_in, second_in,
    act, hidden, terms, dx, dx_in, gate_row, gate_in, back, gate_back, gate_mates,
    local_sem, raw_send, raw_recv, place_send, place_recv, weight_send, weight_recv,
    plane_send, plane_recv, a_send, a_recv, b_send, b_recv, c_send, c_recv, d_send, d_recv,
    dx_send, dx_recv, gate_send, gate_recv, term_send, term_recv, back_send, back_recv,
    mate_send, mate_recv,
):
    rep, me = lax.axis_index("rep"), lax.axis_index("exp")
    plane, q = me // SLICES, me % SLICES
    low, high = q % 2, q // 2
    tok_dev, width = raw.shape[2], raw.shape[3]
    own_rows, hid = w_up.shape
    half, quarter = hid // 2, hid // 4
    items = 2 * planes
    hops = planes - 1
    last_slot = planes + 2 * hops

    def mate(distance):
        return (rep, plane * SLICES + (q + distance) % SLICES)

    def ahead(distance):
        return (rep, (plane + distance) % planes * SLICES + q)

    def behind(distance):
        return (rep, (plane + planes - distance) % planes * SLICES + q)

    def replica(distance):
        return ((rep + distance) % n_rep, me)

    near = (rep, plane * SLICES + high * 2 + 1 - low)
    far = (rep, plane * SLICES + (1 - high) * 2 + low)

    def copy(source, target, send_sem, recv_sem, device):
        return pltpu.make_async_remote_copy(
            src_ref=source, dst_ref=target, send_sem=send_sem, recv_sem=recv_sem,
            device_id=device, device_id_type=MESH,
        )

    def feature_block(index):
        return pl.ds(pl.multiple_of(index * width, 128), width)

    def weight_rows(index):
        return pl.ds(pl.multiple_of(index * own_rows, 16), own_rows)

    def raw_copy(a, j):
        source = (tokens, out_grad)[a]
        return copy(
            source.at[:, feature_block((q + j) % SLICES)], raw.at[a, q],
            raw_send.at[a, j], raw_recv.at[a, j], mate(j),
        )

    def place_copy(j):
        return copy(place.at[q], place.at[q], place_send.at[j], place_recv.at[j], mate(j))

    def weight_copy(a, d):
        source = (w_up, w_down)[a]
        return copy(
            source, weights.at[a, weight_rows(rep)],
            weight_send.at[a, d], weight_recv.at[a, d], replica(d),
        )

    def plane_copy(a, k):
        return copy(
            packed.at[a, k], rows.at[a, k], plane_send.at[a, k], plane_recv.at[a, k], ahead(k)
        )

    def a_copy(s):
        other = pl.ds(pl.multiple_of((1 - low) * half, 128), half)
        return copy(part.at[s, :, other], first_in.at[s], a_send.at[s], a_recv.at[s], near)

    def b_copy(s):
        other = pl.ds(pl.multiple_of((1 - high) * quarter, 128), quarter)
        return copy(first.at[s, :, other], second_in.at[s], b_send.at[s], b_recv.at[s], far)

    own_quarter = pl.ds(pl.multiple_of(low * half + high * quarter, 128), quarter)
    own_half = pl.ds(pl.multiple_of(low * half, 128), half)

    def c_copy(s):
        block = hidden.at[s, :, own_quarter]
        return copy(block, block, c_send.at[s], c_recv.at[s], far)

    def d_copy(s):
        block = hidden.at[s, :, own_half]
        return copy(block, block, d_send.at[s], d_recv.at[s], near)

    def dx_copy(k):
        return copy(dx.at[k], dx_in.at[k], dx_send.at[k], dx_recv.at[k], behind(k))

    def gate_copy(k):
        return copy(gate_row.at[k], gate_in.at[k], gate_send.at[k], gate_recv.at[k], behind(k))

    def term_copy(a, d):
        return copy(
            terms.at[a, weight_rows((rep + d) % n_rep)], (up_sums, down_sums)[a].at[d],
            term_send.at[a, d], term_recv.at[a, d], replica(d),
        )

    def back_copy(j):
        return copy(
            back.at[j], grad_tokens.at[:, feature_block(q)],
            back_send.at[j], back_recv.at[j], mate(j),
        )

    def mate_copy(j):
        return copy(gate_back.at[j], gate_mates.at[j], mate_send.at[j], mate_recv.at[j], mate(j))

    def term_local(a):
        return pltpu.make_async_copy(
            terms.at[a, weight_rows(rep)], (up_sums, down_sums)[a].at[0], local_sem.at[a]
        )

    cot_local = pltpu.make_async_copy(cot, cot_block, local_sem.at[4])
    cot_local.start()
    barrier = pltpu.get_barrier_semaphore()
    peers = [mate(j) for j in range(1, SLICES)] + [replica(d) for d in range(1, n_rep)]
    for device in peers:
        pl.semaphore_signal(barrier, inc=1, device_id=device, device_id_type=MESH)

    @pl.loop(1, planes)
    def _(k):
        pl.semaphore_signal(barrier, inc=1, device_id=ahead(k), device_id_type=MESH)

    pl.semaphore_wait(barrier, len(peers) + planes - 1)

    for j in range(1, SLICES):
        raw_copy(0, j).start()
    for d in range(1, n_rep):
        weight_copy(0, d).start()
    local = [
        pltpu.make_async_copy(tokens.at[:, feature_block(q)], raw.at[0, q], local_sem.at[0]),
        pltpu.make_async_copy(w_up, weights.at[0, weight_rows(rep)], local_sem.at[1]),
        pltpu.make_async_copy(w_down, weights.at[1, weight_rows(rep)], local_sem.at[2]),
    ]
    for c in local:
        c.start()

    route = routes[...]
    count = max(8, planes)
    onehot = (lax.broadcasted_iota(jnp.int32, (count, tok_dev), 0) == route).astype(F32)
    before = (
        lax.broadcasted_iota(jnp.int32, (tok_dev, tok_dev), 0)
        < lax.broadcasted_iota(jnp.int32, (tok_dev, tok_dev), 1)
    ).astype(F32)
    slot = jnp.sum(onehot * dot(onehot, before, (1, 0)), axis=0, keepdims=True)
    position = (route * slots + q * capacity).astype(F32) + slot
    place[q] = jnp.broadcast_to(position, (8, tok_dev))
    for j in range(1, SLICES):
        place_copy(j).start()

    square = lax.broadcasted_iota(jnp.int32, (tok_dev, tok_dev), 0) == lax.broadcasted_iota(
        jnp.int32, (tok_dev, tok_dev), 1
    )
    gate = jnp.sum(jnp.where(square, gates[...], 0.0), axis=1, keepdims=True)
    cot_local.wait()
    for m in range(SLICES):
        block = slice(m * width, (m + 1) * width)
        out_grad[:, block] = (gate * cot_block[:, block].astype(F32)).astype(BF16)
    local_grad = pltpu.make_async_copy(
        out_grad.at[:, feature_block(q)], raw.at[1, q], local_sem.at[3]
    )
    local_grad.start()
    gate_row[...] = jnp.zeros_like(gate_row)

    for j in range(1, SLICES):
        place_copy(j).wait_recv()
    places = jnp.concatenate([place[m, 0:1, :] for m in range(SLICES)], axis=1)

    def chosen(expert, positions, kind):
        number = lax.broadcasted_iota(jnp.int32, (slots, positions.shape[1]), 0) + expert * slots
        return jnp.where(number.astype(F32) == positions, 1.0, 0.0).astype(kind)

    def pack(a, k, target):
        matrix = chosen((plane + k) % planes, places, BF16)
        for start, size in tiles(width):
            source = raw[a, :, :, start : start + size].reshape(SLICES * tok_dev, size)
            target[a, k, :, start : start + size] = dot(matrix, source, (1, 0)).astype(BF16)

    for a in range(2):
        for j in range(1, SLICES):
            sender = (q + SLICES - j) % SLICES
            copy(
                raw.at[a, sender], raw.at[a, sender], raw_send.at[a, j], raw_recv.at[a, j], mate(j)
            ).wait_recv()
        (local[0], local_grad)[a].wait()
        if a == 0:
            for j in range(1, SLICES):
                raw_copy(1, j).start()

        @pl.loop(1, planes)
        def _(k):
            pack(a, k, packed)
            plane_copy(a, k).start()

        pack(a, 0, rows)
    local[1].wait()
    local[2].wait()

    def split(value):
        upper = value.astype(BF16)
        return upper, (value - upper.astype(F32)).astype(BF16)

    def weight_term(a):
        right = hidden[(1 - a) * planes : (2 - a) * planes].reshape(planes * slots, hid)
        for start, size in tiles(width, 512):
            left = rows[a, :, :, start : start + size].reshape(planes * slots, size)
            terms[a, start : start + size, :] = dot(left, right, (0, 0)).astype(BF16)
        for d in range(1, n_rep):
            term_copy(a, d).start()
        term_local(a).start()

    @pl.loop(0, last_slot + 5)
    def _(s):
        def stage(lag):
            slot = s - lag
            extra = slot - planes
            item = jnp.where(extra > 0, planes + extra // 2, slot)
            return item, (slot >= 0) & (slot <= last_slot) & ((extra <= 0) | (extra % 2 == 0))

        e_item, e_here = stage(4)

        @pl.when(e_here)
        def _():
            t = e_item
            landed = hidden.at[t, :, pl.ds(pl.multiple_of((1 - low) * half, 128), half)]
            copy(landed, landed, d_send.at[t], d_recv.at[t], near).wait_recv()

            @pl.when(t >= planes)
            def _():
                k = t - planes
                left = hidden[t]
                for start, size in tiles(width):
                    dx[k, :, start : start + size] = dot(
                        left, weights[0, start : start + size, :], (1, 1)
                    ).astype(BF16)

                @pl.when(k > 0)
                def _():
                    gate_copy(k).start()
                    dx_copy(k).start()

        d_item, d_here = stage(3)

        @pl.when(d_here)
        def _():
            t = d_item
            landed = hidden.at[
                t, :, pl.ds(pl.multiple_of(low * half + (1 - high) * quarter, 128), quarter)
            ]
            copy(landed, landed, c_send.at[t], c_recv.at[t], far).wait_recv()
            d_copy(t).start()

        c_item, c_here = stage(2)

        @pl.when(c_here)
        def _():
            t = c_item
            b_copy(t).wait_recv()
            mine = pl.ds(pl.multiple_of(high * quarter, 128), quarter)
            total = first[t, :, mine].astype(F32) + second_in[t].astype(F32)

            @pl.when(t < planes)
            def _():
                act[t] = total
                hidden[t, :, own_quarter] = (total * jax.nn.sigmoid(total)).astype(BF16)

            @pl.when(t >= planes)
            def _():
                k = t - planes
                value = act[k]
                gating = jax.nn.sigmoid(value)
                hidden[t, :, own_quarter] = (
                    total * gating * (1.0 + value * (1.0 - gating))
                ).astype(BF16)
                upper, lower = split(total * (value * gating))
                ones = jnp.ones((16, quarter), BF16)
                sums = dot(ones, upper, (1, 1)) + dot(ones, lower, (1, 1))
                gate_row[k, :, 0:slots] = sums[0:8]

            c_copy(t).start()

        b_item, b_here = stage(1)

        @pl.when(b_here)
        def _():
            t = b_item
            a_copy(t).wait_recv()
            first[t] = (part[t, :, own_half].astype(F32) + first_in[t].astype(F32)).astype(BF16)
            b_copy(t).start()

        i, here = stage(0)

        @pl.when(here)
        def _():
            a, k = i // planes, i % planes

            @pl.when(k == 0)
            def _():
                for d in range(1, n_rep):
                    landed = weights.at[a, weight_rows((rep + n_rep - d) % n_rep)]
                    copy(
                        landed, landed, weight_send.at[a, d], weight_recv.at[a, d], replica(d)
                    ).wait_recv()

                @pl.when(a == 0)
                def _():
                    for d in range(1, n_rep):
                        weight_copy(1, d).start()

            @pl.when(k > 0)
            def _():
                plane_copy(a, k).wait_recv()

            left = rows[a, k]
            for start, size in tiles(hid):
                part[i, :, start : start + size] = dot(
                    left, weights[a, :, start : start + size], (1, 0)
                ).astype(BF16)
            a_copy(i).start()

        @pl.when(s == last_slot + 1)
        def _():
            weight_term(1)

    weight_term(0)

    @pl.loop(1, planes)
    def _(k):
        gate_copy(k).wait_recv()
        dx_copy(k).wait_recv()

    for j in (2, 1, 3, 0):
        positions = place[(q + j) % SLICES][0:1, :]
        blocks = [chosen((plane + k) % planes, positions, BF16) for k in range(planes)]
        matrix = jnp.concatenate(blocks, axis=0)
        for start, size in tiles(width):
            landed = jnp.concatenate(
                [dx[0, :, start : start + size]]
                + [dx_in[k, :, start : start + size] for k in range(1, planes)],
                axis=0,
            )
            back[j, :, start : start + size] = dot(matrix, landed, (0, 0)).astype(BF16)
        sums = jnp.zeros((8, tok_dev), F32)
        for k in range(planes):
            upper, lower = split((gate_row if k == 0 else gate_in)[k, :, 0:slots])
            both = dot(jnp.concatenate([upper, lower], axis=0), blocks[k], (1, 0))
            sums += both[0:8] + both[8:16]
        gate_back[j] = sums
        if j > 0:
            back_copy(j).start()
            mate_copy(j).start()
    last = pltpu.make_async_copy(
        back.at[0], grad_tokens.at[:, feature_block(q)], local_sem.at[2]
    )
    last.start()
    total = gate_back[0]
    for j in range(1, SLICES):
        mate_copy(j).wait_recv()
        total += gate_mates[j]
    gate_sums[...] = total[0:1] / gates[...]
    last.wait()
    for j in range(1, SLICES):
        landed = grad_tokens.at[:, feature_block((q + SLICES - j) % SLICES)]
        copy(landed, landed, back_send.at[j], back_recv.at[j], mate(j)).wait_recv()
    for a in range(2):
        term_local(a).wait()
        for d in range(1, n_rep):
            term_copy(a, d).wait_recv()
            term_copy(a, d).wait_send()
            weight_copy(a, d).wait_send()
        for j in range(1, SLICES):
            raw_copy(a, j).wait_send()

        @pl.loop(1, planes)
        def _(k):
            plane_copy(a, k).wait_send()

    for j in range(1, SLICES):
        place_copy(j).wait_send()
        back_copy(j).wait_send()
        mate_copy(j).wait_send()

    @pl.loop(1, planes)
    def _(k):
        dx_copy(k).wait_send()
        gate_copy(k).wait_send()

    @pl.loop(0, items)
    def _(s):
        a_copy(s).wait_send()
        b_copy(s).wait_send()
        c_copy(s).wait_send()
        d_copy(s).wait_send()


def shards(tokens, cotangent, gates, routes, w_up, w_down_t):
    tok_dev, top_count = routes.shape
    model_width = tokens.shape[1]
    width = model_width // SLICES
    n_rep, n_exp = lax.axis_size("rep"), lax.axis_size("exp")
    planes = n_exp // SLICES
    capacity = min(tok_dev, max(2, 9 * tok_dev * top_count // (8 * planes)))
    slots = -(-SLICES * capacity // 16) * 16
    lanes = -(-slots // 128) * 128
    own_rows, hid = w_up.shape
    items = 2 * planes
    dma = pltpu.SemaphoreType.DMA
    vmem = pl.BlockSpec(memory_space=pltpu.VMEM)
    hbm = pl.BlockSpec(memory_space=pl.ANY)
    pairs = []
    for shape in (
        (2, SLICES), (SLICES,), (2, n_rep), (2, planes), (items,), (items,), (items,), (items,),
        (planes,), (planes,), (2, n_rep), (SLICES,), (SLICES,),
    ):
        pairs += [dma(shape), dma(shape)]
    grad_tokens, gate_sums, up_sums, down_sums = pl.pallas_call(
        functools.partial(kernel, n_rep, planes, capacity, slots),
        out_shape=(
            jax.ShapeDtypeStruct((tok_dev, model_width), BF16),
            jax.ShapeDtypeStruct((1, tok_dev), F32),
            jax.ShapeDtypeStruct((n_rep, own_rows, hid), BF16),
            jax.ShapeDtypeStruct((n_rep, own_rows, hid), BF16),
        ),
        in_specs=[hbm, hbm, vmem, vmem, hbm, hbm],
        out_specs=(hbm, vmem, hbm, hbm),
        scratch_shapes=[
            pltpu.VMEM((tok_dev, model_width), BF16),
            pltpu.VMEM((tok_dev, model_width), BF16),
            pltpu.VMEM((2, SLICES, tok_dev, width), BF16),
            pltpu.VMEM((SLICES, 8, tok_dev), F32),
            pltpu.VMEM((2, width, hid), BF16),
            pltpu.VMEM((2, planes, slots, width), BF16),
            pltpu.VMEM((2, planes, slots, width), BF16),
            pltpu.VMEM((items, slots, hid), BF16),
            pltpu.VMEM((items, slots, hid // 2), BF16),
            pltpu.VMEM((items, slots, hid // 2), BF16),
            pltpu.VMEM((items, slots, hid // 4), BF16),
            pltpu.VMEM((planes, slots, hid // 4), F32),
            pltpu.VMEM((items, slots, hid), BF16),
            pltpu.VMEM((2, width, hid), BF16),
            pltpu.VMEM((planes, slots, width), BF16),
            pltpu.VMEM((planes, slots, width), BF16),
            pltpu.VMEM((planes, 8, lanes), F32),
            pltpu.VMEM((planes, 8, lanes), F32),
            pltpu.VMEM((SLICES, tok_dev, width), BF16),
            pltpu.VMEM((SLICES, 8, tok_dev), F32),
            pltpu.VMEM((SLICES, 8, tok_dev), F32),
            dma((5,)),
            *pairs,
        ],
        compiler_params=pltpu.CompilerParams(
            collective_id=0, has_side_effects=True, vmem_limit_bytes=56 * 1024 * 1024
        ),
        cost_estimate=pl.CostEstimate(
            flops=12 * planes * slots * width * hid, bytes_accessed=8 * 1024 * 1024, transcendentals=0
        ),
    )(tokens, cotangent, gates.reshape(1, tok_dev), routes.reshape(1, tok_dev), w_up, w_down_t)
    grad_up = sum(up_sums[d].astype(F32) for d in range(n_rep))
    grad_down_t = sum(down_sums[d].astype(F32) for d in range(n_rep))
    return grad_tokens, gate_sums.reshape(tok_dev, top_count), grad_up, grad_down_t


def solution(mesh):
    split = P(("rep", "exp"), None)
    weight_split = P(("exp", "rep"), None)
    return jax.shard_map(
        shards,
        mesh=mesh,
        in_specs=(split, split, split, split, weight_split, weight_split),
        out_specs=(split, split, weight_split, weight_split),
        check_vma=False,
    )
```

```python
import functools

import jax
import jax.numpy as jnp
from jax import lax
from jax.experimental import pallas as pl
from jax.experimental.pallas import tpu as pltpu
from jax.sharding import PartitionSpec as P

SLICES = 4
MESH = pl.DeviceIdType.MESH
F32, BF16 = jnp.float32, jnp.bfloat16


def dot(left, right, dims, precision=None):
    return lax.dot_general(
        left, right, ((dims[:1], dims[1:]), ((), ())), preferred_element_type=F32, precision=precision
    )


def tiles(width, step=256):
    return [(start, min(step, width - start)) for start in range(0, width, step)]


def kernel(
    n_rep, planes, capacity, slots, pair, cover,
    tokens, cot, gates, routes, w_up, w_down,
    grad_tokens, gate_sums, up_sums, down_sums,
    cot_block, out_grad, raw, place, weights, packed, rows, part, first, first_in, second_in,
    act, hidden, terms, dx, dx_in, gate_row, gate_in, back, gate_back, gate_mates,
    rows_peer, hidden_peer,
    local_sem, raw_send, raw_recv, place_send, place_recv, weight_send, weight_recv,
    plane_send, plane_recv, a_send, a_recv, b_send, b_recv, c_send, c_recv, d_send, d_recv,
    dx_send, dx_recv, gate_send, gate_recv, term_send, term_recv, back_send, back_recv,
    mate_send, mate_recv, y_send, y_recv, h_send, h_recv, f_send, f_recv, g_send, g_recv,
):
    rep, me = lax.axis_index("rep"), lax.axis_index("exp")
    plane, q = me // SLICES, me % SLICES
    low, high = q % 2, q // 2
    tok_dev, width = raw.shape[2], raw.shape[3]
    own_rows, hid = w_up.shape
    half, quarter = hid // 2, hid // 4
    items = 2 * planes
    hops = planes - 1
    parts = tiles(width, 512)
    last_slot = planes + 2 * hops

    def mate(distance):
        return (rep, plane * SLICES + (q + distance) % SLICES)

    def ahead(distance):
        return (rep, (plane + distance) % planes * SLICES + q)

    def behind(distance):
        return (rep, (plane + planes - distance) % planes * SLICES + q)

    def replica(distance):
        return ((rep + distance) % n_rep, me)

    near = (rep, plane * SLICES + high * 2 + 1 - low)
    far = (rep, plane * SLICES + (1 - high) * 2 + low)

    def copy(source, target, send_sem, recv_sem, device):
        return pltpu.make_async_remote_copy(
            src_ref=source, dst_ref=target, send_sem=send_sem, recv_sem=recv_sem,
            device_id=device, device_id_type=MESH,
        )

    def feature_block(index):
        return pl.ds(pl.multiple_of(index * width, 128), width)

    def weight_rows(index):
        return pl.ds(pl.multiple_of(index * own_rows, 16), own_rows)

    def feature_part(index, p):
        start, size = parts[p]
        return pl.ds(pl.multiple_of(index * width + start, 128), size)

    def inner(p):
        start, size = parts[p]
        return slice(start, start + size)

    def raw_copy(a, j, p):
        source = (tokens, out_grad)[a]
        return copy(
            source.at[:, feature_part((q + j) % SLICES, p)], raw.at[a, q, :, inner(p)],
            raw_send.at[a, p, j], raw_recv.at[a, p, j], mate(j),
        )

    def place_copy(j):
        return copy(place.at[q], place.at[q], place_send.at[j], place_recv.at[j], mate(j))

    def weight_copy(a, d):
        source = (w_up, w_down)[a]
        return copy(
            source, weights.at[a, weight_rows(rep)],
            weight_send.at[a, d], weight_recv.at[a, d], replica(d),
        )

    def plane_copy(a, k, p):
        return copy(
            packed.at[a, k, :, inner(p)], rows.at[a, k, :, inner(p)],
            plane_send.at[a, p, k], plane_recv.at[a, p, k], ahead(k),
        )

    def a_copy(s):
        other = pl.ds(pl.multiple_of((1 - low) * half, 128), half)
        return copy(part.at[s, :, other], first_in.at[s], a_send.at[s], a_recv.at[s], near)

    def b_copy(s):
        other = pl.ds(pl.multiple_of((1 - high) * quarter, 128), quarter)
        return copy(first.at[s, :, other], second_in.at[s], b_send.at[s], b_recv.at[s], far)

    own_quarter = pl.ds(pl.multiple_of(low * half + high * quarter, 128), quarter)
    own_half = pl.ds(pl.multiple_of(low * half, 128), half)

    def c_copy(s):
        block = hidden.at[s, :, own_quarter]
        return copy(block, block, c_send.at[s], c_recv.at[s], far)

    def d_copy(s):
        block = hidden.at[s, :, own_half]
        return copy(block, block, d_send.at[s], d_recv.at[s], near)

    def dx_copy(k, p):
        return copy(
            dx.at[k, :, inner(p)], dx_in.at[k, :, inner(p)],
            dx_send.at[p, k], dx_recv.at[p, k], behind(k),
        )

    def cover_start(replica_index):
        return jnp.minimum(replica_index * own_rows // 128 * 128, width - cover)

    def y_copy(a, k):
        block = pl.ds(pl.multiple_of(cover_start((rep + 1) % n_rep), 128), cover)
        return copy(
            rows.at[a, k, :, block], rows_peer.at[a, k], y_send.at[a, k], y_recv.at[a, k], replica(1)
        )

    def h_copy(t):
        return copy(
            hidden.at[t, :, own_quarter], hidden_peer.at[t, :, own_quarter],
            h_send.at[t], h_recv.at[t], replica(1),
        )

    def f_copy(t):
        block = hidden_peer.at[t, :, own_quarter]
        return copy(block, block, f_send.at[t], f_recv.at[t], far)

    def g_copy(t):
        block = hidden_peer.at[t, :, own_half]
        return copy(block, block, g_send.at[t], g_recv.at[t], near)

    def gate_copy(k):
        return copy(gate_row.at[k], gate_in.at[k], gate_send.at[k], gate_recv.at[k], behind(k))

    def term_copy(a, d):
        return copy(
            terms.at[a, weight_rows((rep + d) % n_rep)], (up_sums, down_sums)[a].at[d],
            term_send.at[a, d], term_recv.at[a, d], replica(d),
        )

    def back_copy(j, p):
        return copy(
            back.at[j, :, inner(p)], grad_tokens.at[:, feature_part(q, p)],
            back_send.at[p, j], back_recv.at[p, j], mate(j),
        )

    def mate_copy(j):
        return copy(gate_back.at[j], gate_mates.at[j], mate_send.at[j], mate_recv.at[j], mate(j))

    def term_local(a):
        kept = weight_rows(rep)
        if pair:
            kept = pl.ds(pl.multiple_of(rep * own_rows - cover_start(rep), 16), own_rows)
        return pltpu.make_async_copy(
            terms.at[a, kept], (up_sums, down_sums)[a].at[0], local_sem.at[a]
        )

    cot_local = pltpu.make_async_copy(cot, cot_block, local_sem.at[4])
    cot_local.start()
    barrier = pltpu.get_barrier_semaphore()
    peers = [mate(j) for j in range(1, SLICES)] + [replica(d) for d in range(1, n_rep)]
    for device in peers:
        pl.semaphore_signal(barrier, inc=1, device_id=device, device_id_type=MESH)

    @pl.loop(1, planes)
    def _(k):
        pl.semaphore_signal(barrier, inc=1, device_id=ahead(k), device_id_type=MESH)

    pl.semaphore_wait(barrier, len(peers) + planes - 1)

    for j in range(1, SLICES):
        raw_copy(0, j, 0).start()
    for d in range(1, n_rep):
        weight_copy(0, d).start()
    local = [
        pltpu.make_async_copy(tokens.at[:, feature_block(q)], raw.at[0, q], local_sem.at[0]),
        pltpu.make_async_copy(w_up, weights.at[0, weight_rows(rep)], local_sem.at[1]),
        pltpu.make_async_copy(w_down, weights.at[1, weight_rows(rep)], local_sem.at[2]),
    ]
    for c in local:
        c.start()

    route = routes[...]
    count = max(8, planes)
    onehot = (lax.broadcasted_iota(jnp.int32, (count, tok_dev), 0) == route).astype(F32)
    before = (
        lax.broadcasted_iota(jnp.int32, (tok_dev, tok_dev), 0)
        < lax.broadcasted_iota(jnp.int32, (tok_dev, tok_dev), 1)
    ).astype(F32)
    slot = jnp.sum(onehot * dot(onehot, before, (1, 0)), axis=0, keepdims=True)
    position = (route * slots + q * capacity).astype(F32) + slot
    place[q] = jnp.broadcast_to(position, (8, tok_dev))
    for j in range(1, SLICES):
        place_copy(j).start()
    for p in range(1, len(parts)):
        for j in range(1, SLICES):
            raw_copy(0, j, p).start()

    square = lax.broadcasted_iota(jnp.int32, (tok_dev, tok_dev), 0) == lax.broadcasted_iota(
        jnp.int32, (tok_dev, tok_dev), 1
    )
    gate = jnp.sum(jnp.where(square, gates[...], 0.0), axis=1, keepdims=True)
    cot_local.wait()
    for m in range(SLICES):
        block = slice(m * width, (m + 1) * width)
        out_grad[:, block] = (gate * cot_block[:, block].astype(F32)).astype(BF16)
    local_grad = pltpu.make_async_copy(
        out_grad.at[:, feature_block(q)], raw.at[1, q], local_sem.at[3]
    )
    local_grad.start()
    gate_row[...] = jnp.zeros_like(gate_row)

    for j in range(1, SLICES):
        place_copy(j).wait_recv()
    places = jnp.concatenate([place[m, 0:1, :] for m in range(SLICES)], axis=1)

    def chosen(expert, positions, kind):
        number = lax.broadcasted_iota(jnp.int32, (slots, positions.shape[1]), 0) + expert * slots
        return jnp.where(number.astype(F32) == positions, 1.0, 0.0).astype(kind)

    def pack(a, k, p, target):
        matrix = chosen((plane + k) % planes, places, BF16)
        begin, length = parts[p]
        for start, size in tiles(length):
            block = slice(begin + start, begin + start + size)
            source = raw[a, :, :, block].reshape(SLICES * tok_dev, size)
            target[a, k, :, block] = dot(matrix, source, (1, 0)).astype(BF16)

    for a in range(2):
        (local[0], local_grad)[a].wait()
        for p in range(len(parts)):
            for j in range(1, SLICES):
                landed = raw.at[a, (q + SLICES - j) % SLICES, :, inner(p)]
                copy(
                    landed, landed, raw_send.at[a, p, j], raw_recv.at[a, p, j], mate(j)
                ).wait_recv()
            if a == 0:
                for j in range(1, SLICES):
                    raw_copy(1, j, p).start()

            @pl.loop(1, planes)
            def _(k):
                pack(a, k, p, packed)
                plane_copy(a, k, p).start()

            pack(a, 0, p, rows)
        if pair:
            y_copy(a, 0).start()
    local[1].wait()
    local[2].wait()

    def dx_product(k, p):
        left = hidden[planes + k]
        begin, length = parts[p]
        for start, size in tiles(length):
            block = slice(begin + start, begin + start + size)
            dx[k, :, block] = dot(left, weights[0, block, :], (1, 1)).astype(BF16)

    def split(value):
        upper = value.astype(BF16)
        return upper, (value - upper.astype(F32)).astype(BF16)

    def weight_term(a):
        right = hidden[(1 - a) * planes : (2 - a) * planes].reshape(planes * slots, hid)
        for start, size in tiles(width, 512):
            left = rows[a, :, :, start : start + size].reshape(planes * slots, size)
            terms[a, start : start + size, :] = dot(left, right, (0, 0)).astype(BF16)
        for d in range(1, n_rep):
            term_copy(a, d).start()
        term_local(a).start()

    @pl.loop(0, last_slot + (9 if pair else 6))
    def _(s):
        def stage(lag):
            slot = s - lag
            extra = slot - planes
            item = jnp.where(extra > 0, planes + extra // 2, slot)
            return item, (slot >= 0) & (slot <= last_slot) & ((extra <= 0) | (extra % 2 == 0))

        e_item, e_here = stage(4)

        @pl.when(e_here)
        def _():
            t = e_item
            landed = hidden.at[t, :, pl.ds(pl.multiple_of((1 - low) * half, 128), half)]
            copy(landed, landed, d_send.at[t], d_recv.at[t], near).wait_recv()

            @pl.when(t >= planes)
            def _():
                k = t - planes
                dx_product(k, 0)

                @pl.when(k > 0)
                def _():
                    gate_copy(k).start()
                    dx_copy(k, 0).start()

        d_item, d_here = stage(3)

        @pl.when(d_here)
        def _():
            t = d_item
            landed = hidden.at[
                t, :, pl.ds(pl.multiple_of(low * half + (1 - high) * quarter, 128), quarter)
            ]
            copy(landed, landed, c_send.at[t], c_recv.at[t], far).wait_recv()
            d_copy(t).start()

        c_item, c_here = stage(2)

        @pl.when(c_here)
        def _():
            t = c_item
            b_copy(t).wait_recv()
            mine = pl.ds(pl.multiple_of(high * quarter, 128), quarter)
            total = first[t, :, mine].astype(F32) + second_in[t].astype(F32)

            @pl.when(t < planes)
            def _():
                act[t] = total
                hidden[t, :, own_quarter] = (total * jax.nn.sigmoid(total)).astype(BF16)

            @pl.when(t >= planes)
            def _():
                k = t - planes
                value = act[k]
                gating = jax.nn.sigmoid(value)
                hidden[t, :, own_quarter] = (
                    total * gating * (1.0 + value * (1.0 - gating))
                ).astype(BF16)
                upper, lower = split(total * (value * gating))
                ones = jnp.ones((16, quarter), BF16)
                sums = dot(ones, upper, (1, 1)) + dot(ones, lower, (1, 1))
                gate_row[k, :, 0:slots] = sums[0:8]

            c_copy(t).start()
            if pair:
                h_copy(t).start()

        b_item, b_here = stage(1)

        @pl.when(b_here)
        def _():
            t = b_item
            a_copy(t).wait_recv()
            first[t] = (part[t, :, own_half].astype(F32) + first_in[t].astype(F32)).astype(BF16)
            b_copy(t).start()

        i, here = stage(0)

        @pl.when(here)
        def _():
            a, k = i // planes, i % planes

            @pl.when(k == 0)
            def _():
                for d in range(1, n_rep):
                    landed = weights.at[a, weight_rows((rep + n_rep - d) % n_rep)]
                    copy(
                        landed, landed, weight_send.at[a, d], weight_recv.at[a, d], replica(d)
                    ).wait_recv()

                @pl.when(a == 0)
                def _():
                    for d in range(1, n_rep):
                        weight_copy(1, d).start()

            @pl.when(k > 0)
            def _():
                for p in range(len(parts)):
                    plane_copy(a, k, p).wait_recv()
                if pair:
                    y_copy(a, k).start()

            left = rows[a, k]
            for start, size in tiles(hid):
                part[i, :, start : start + size] = dot(
                    left, weights[a, :, start : start + size], (1, 0)
                ).astype(BF16)
            a_copy(i).start()

        @pl.when(s == last_slot + 5)
        def _():
            for p in range(1, len(parts)):
                dx_product(0, p)

                @pl.loop(1, planes)
                def _(k):
                    dx_product(k, p)
                    dx_copy(k, p).start()

        if pair:
            f_item, f_here = stage(6)

            @pl.when(f_here)
            def _():
                h_copy(f_item).wait_recv()
                f_copy(f_item).start()

            g_item, g_here = stage(8)

            @pl.when(g_here)
            def _():
                t = g_item
                landed = hidden_peer.at[
                    t, :, pl.ds(pl.multiple_of(low * half + (1 - high) * quarter, 128), quarter)
                ]
                copy(landed, landed, f_send.at[t], f_recv.at[t], far).wait_recv()
                g_copy(t).start()
        else:
            @pl.when(s == last_slot + 1)
            def _():
                weight_term(1)

    def pair_term(a):
        @pl.loop((1 - a) * planes, (2 - a) * planes)
        def _(t):
            landed = hidden_peer.at[t, :, pl.ds(pl.multiple_of((1 - low) * half, 128), half)]
            copy(landed, landed, g_send.at[t], g_recv.at[t], near).wait_recv()

        @pl.loop(0, planes)
        def _(k):
            landed = rows_peer.at[a, k]
            copy(landed, landed, y_send.at[a, k], y_recv.at[a, k], replica(1)).wait_recv()

        count = planes * slots
        mine = pl.ds(pl.multiple_of(cover_start(rep), 128), cover)
        some = slice((1 - a) * planes, (2 - a) * planes)
        total = dot(
            rows[a, :, :, mine].reshape(count, cover), hidden[some].reshape(count, hid), (0, 0)
        )
        total += dot(
            rows_peer[a].reshape(count, cover), hidden_peer[some].reshape(count, hid), (0, 0)
        )
        terms[a] = total.astype(BF16)
        term_local(a).start()

    if pair:
        pair_term(1)
        pair_term(0)
    else:
        weight_term(0)

    @pl.loop(1, planes)
    def _(k):
        gate_copy(k).wait_recv()

    for p in range(len(parts)):
        @pl.loop(1, planes)
        def _(k):
            dx_copy(k, p).wait_recv()

        for j in (2, 1, 3, 0):
            positions = place[(q + j) % SLICES][0:1, :]
            blocks = [chosen((plane + k) % planes, positions, BF16) for k in range(planes)]
            matrix = jnp.concatenate(blocks, axis=0)
            landed = jnp.concatenate(
                [dx[0, :, inner(p)]] + [dx_in[k, :, inner(p)] for k in range(1, planes)], axis=0
            )
            back[j, :, inner(p)] = dot(matrix, landed, (0, 0)).astype(BF16)
            if j > 0:
                back_copy(j, p).start()
            if p > 0:
                continue
            sums = jnp.zeros((8, tok_dev), F32)
            for k in range(planes):
                upper, lower = split((gate_row if k == 0 else gate_in)[k, :, 0:slots])
                both = dot(jnp.concatenate([upper, lower], axis=0), blocks[k], (1, 0))
                sums += both[0:8] + both[8:16]
            gate_back[j] = sums
            if j > 0:
                mate_copy(j).start()
    last = pltpu.make_async_copy(
        back.at[0], grad_tokens.at[:, feature_block(q)], local_sem.at[2]
    )
    last.start()
    total = gate_back[0]
    for j in range(1, SLICES):
        mate_copy(j).wait_recv()
        total += gate_mates[j]
    gate_sums[...] = total[0:1] / gates[...]
    last.wait()
    for p in range(len(parts)):
        for j in range(1, SLICES):
            landed = grad_tokens.at[:, feature_part((q + SLICES - j) % SLICES, p)]
            copy(landed, landed, back_send.at[p, j], back_recv.at[p, j], mate(j)).wait_recv()
            back_copy(j, p).wait_send()
    for a in range(2):
        term_local(a).wait()
        for d in range(1, n_rep):
            if not pair:
                term_copy(a, d).wait_recv()
                term_copy(a, d).wait_send()
            weight_copy(a, d).wait_send()
        for j in range(1, SLICES):
            for p in range(len(parts)):
                raw_copy(a, j, p).wait_send()

        @pl.loop(1, planes)
        def _(k):
            for p in range(len(parts)):
                plane_copy(a, k, p).wait_send()

    for j in range(1, SLICES):
        place_copy(j).wait_send()
        mate_copy(j).wait_send()

    @pl.loop(1, planes)
    def _(k):
        for p in range(len(parts)):
            dx_copy(k, p).wait_send()
        gate_copy(k).wait_send()

    @pl.loop(0, items)
    def _(s):
        a_copy(s).wait_send()
        b_copy(s).wait_send()
        c_copy(s).wait_send()
        d_copy(s).wait_send()
        if pair:
            h_copy(s).wait_send()
            f_copy(s).wait_send()
            g_copy(s).wait_send()
            y_copy(s // planes, s % planes).wait_send()


def shards(tokens, cotangent, gates, routes, w_up, w_down_t):
    tok_dev, top_count = routes.shape
    model_width = tokens.shape[1]
    width = model_width // SLICES
    n_rep, n_exp = lax.axis_size("rep"), lax.axis_size("exp")
    planes = n_exp // SLICES
    capacity = min(tok_dev, max(2, 9 * tok_dev * top_count // (8 * planes)))
    slots = -(-SLICES * capacity // 16) * 16
    lanes = -(-slots // 128) * 128
    own_rows, hid = w_up.shape
    items = 2 * planes
    pair = n_rep == 2
    cover = max(
        -(-(r + 1) * own_rows // 128) * 128 - r * own_rows // 128 * 128 for r in range(n_rep)
    )
    sums = 1 if pair else n_rep
    peer = planes if pair else 1
    n_parts = len(tiles(width, 512))
    dma = pltpu.SemaphoreType.DMA
    vmem = pl.BlockSpec(memory_space=pltpu.VMEM)
    hbm = pl.BlockSpec(memory_space=pl.ANY)
    pairs = []
    for shape in (
        (2, n_parts, SLICES), (SLICES,), (2, n_rep), (2, n_parts, planes), (items,), (items,), (items,), (items,),
        (n_parts, planes), (planes,), (2, n_rep), (n_parts, SLICES), (SLICES,),
        (2, planes), (items,), (items,), (items,),
    ):
        pairs += [dma(shape), dma(shape)]
    grad_tokens, gate_sums, up_sums, down_sums = pl.pallas_call(
        functools.partial(kernel, n_rep, planes, capacity, slots, pair, cover),
        out_shape=(
            jax.ShapeDtypeStruct((tok_dev, model_width), BF16),
            jax.ShapeDtypeStruct((1, tok_dev), F32),
            jax.ShapeDtypeStruct((sums, own_rows, hid), BF16),
            jax.ShapeDtypeStruct((sums, own_rows, hid), BF16),
        ),
        in_specs=[hbm, hbm, vmem, vmem, hbm, hbm],
        out_specs=(hbm, vmem, hbm, hbm),
        scratch_shapes=[
            pltpu.VMEM((tok_dev, model_width), BF16),
            pltpu.VMEM((tok_dev, model_width), BF16),
            pltpu.VMEM((2, SLICES, tok_dev, width), BF16),
            pltpu.VMEM((SLICES, 8, tok_dev), F32),
            pltpu.VMEM((2, width, hid), BF16),
            pltpu.VMEM((2, planes, slots, width), BF16),
            pltpu.VMEM((2, planes, slots, width), BF16),
            pltpu.VMEM((items, slots, hid), BF16),
            pltpu.VMEM((items, slots, hid // 2), BF16),
            pltpu.VMEM((items, slots, hid // 2), BF16),
            pltpu.VMEM((items, slots, hid // 4), BF16),
            pltpu.VMEM((planes, slots, hid // 4), F32),
            pltpu.VMEM((items, slots, hid), BF16),
            pltpu.VMEM((2, cover if pair else width, hid), BF16),
            pltpu.VMEM((planes, slots, width), BF16),
            pltpu.VMEM((planes, slots, width), BF16),
            pltpu.VMEM((planes, 8, lanes), F32),
            pltpu.VMEM((planes, 8, lanes), F32),
            pltpu.VMEM((SLICES, tok_dev, width), BF16),
            pltpu.VMEM((SLICES, 8, tok_dev), F32),
            pltpu.VMEM((SLICES, 8, tok_dev), F32),
            pltpu.VMEM((2, peer, slots, cover), BF16),
            pltpu.VMEM((2 * peer, slots, hid), BF16),
            dma((5,)),
            *pairs,
        ],
        compiler_params=pltpu.CompilerParams(
            collective_id=0, has_side_effects=True, vmem_limit_bytes=56 * 1024 * 1024
        ),
        cost_estimate=pl.CostEstimate(
            flops=12 * planes * slots * width * hid, bytes_accessed=8 * 1024 * 1024, transcendentals=0
        ),
    )(tokens, cotangent, gates.reshape(1, tok_dev), routes.reshape(1, tok_dev), w_up, w_down_t)
    grad_up = sum(up_sums[d].astype(F32) for d in range(sums))
    grad_down_t = sum(down_sums[d].astype(F32) for d in range(sums))
    return grad_tokens, gate_sums.reshape(tok_dev, top_count), grad_up, grad_down_t


def solution(mesh):
    split = P(("rep", "exp"), None)
    weight_split = P(("exp", "rep"), None)
    return jax.shard_map(
        shards,
        mesh=mesh,
        in_specs=(split, split, split, split, weight_split, weight_split),
        out_specs=(split, split, weight_split, weight_split),
        check_vma=False,
    )
```

```python
import functools

import jax
import jax.numpy as jnp
from jax import lax
from jax.experimental import pallas as pl
from jax.experimental.pallas import tpu as pltpu
from jax.sharding import PartitionSpec as P

SLICES = 4
MESH = pl.DeviceIdType.MESH
F32, BF16 = jnp.float32, jnp.bfloat16


def dot(left, right, dims, precision=None):
    return lax.dot_general(
        left, right, ((dims[:1], dims[1:]), ((), ())), preferred_element_type=F32, precision=precision
    )


def tiles(width, step=256):
    return [(start, min(step, width - start)) for start in range(0, width, step)]


def kernel(
    n_rep, planes, capacity, slots, pair, cover,
    tokens, cot, gates, routes, w_up, w_down,
    grad_tokens, gate_sums, up_sums, down_sums,
    cot_block, out_grad, raw, place, weights, packed, rows, part, first, first_in, second_in,
    act, hidden, terms, dx, dx_in, gate_row, gate_in, back, gate_back, gate_mates,
    rows_peer, hidden_peer, matrix,
    local_sem, raw_send, raw_recv, place_send, place_recv, weight_send, weight_recv,
    plane_send, plane_recv, a_send, a_recv, b_send, b_recv, c_send, c_recv, d_send, d_recv,
    dx_send, dx_recv, gate_send, gate_recv, term_send, term_recv, back_send, back_recv,
    mate_send, mate_recv, y_send, y_recv, h_send, h_recv, f_send, f_recv, g_send, g_recv,
):
    rep, me = lax.axis_index("rep"), lax.axis_index("exp")
    plane, q = me // SLICES, me % SLICES
    low, high = q % 2, q // 2
    tok_dev, width = raw.shape[2], raw.shape[3]
    own_rows, hid = w_up.shape
    half, quarter = hid // 2, hid // 4
    items = 2 * planes
    hops = planes - 1
    parts = tiles(width, 512)
    early = 2 * hops
    last_slot = early + 5

    def mate(distance):
        return (rep, plane * SLICES + (q + distance) % SLICES)

    def ahead(distance):
        return (rep, (plane + distance) % planes * SLICES + q)

    def behind(distance):
        return (rep, (plane + planes - distance) % planes * SLICES + q)

    def replica(distance):
        return ((rep + distance) % n_rep, me)

    near = (rep, plane * SLICES + high * 2 + 1 - low)
    far = (rep, plane * SLICES + (1 - high) * 2 + low)

    def copy(source, target, send_sem, recv_sem, device):
        return pltpu.make_async_remote_copy(
            src_ref=source, dst_ref=target, send_sem=send_sem, recv_sem=recv_sem,
            device_id=device, device_id_type=MESH,
        )

    def feature_block(index):
        return pl.ds(pl.multiple_of(index * width, 128), width)

    def weight_rows(index):
        return pl.ds(pl.multiple_of(index * own_rows, 16), own_rows)

    def feature_part(index, p):
        start, size = parts[p]
        return pl.ds(pl.multiple_of(index * width + start, 128), size)

    def inner(p):
        start, size = parts[p]
        return slice(start, start + size)

    def raw_copy(a, j, p):
        source = (tokens, out_grad)[a]
        return copy(
            source.at[:, feature_part((q + j) % SLICES, p)], raw.at[a, q, :, inner(p)],
            raw_send.at[a, p, j], raw_recv.at[a, p, j], mate(j),
        )

    def place_copy(j):
        return copy(place.at[q], place.at[q], place_send.at[j], place_recv.at[j], mate(j))

    def weight_copy(a, d):
        source = (w_up, w_down)[a]
        return copy(
            source, weights.at[a, weight_rows(rep)],
            weight_send.at[a, d], weight_recv.at[a, d], replica(d),
        )

    def plane_copy(a, k, p):
        return copy(
            packed.at[a, k, :, inner(p)], rows.at[a, k, :, inner(p)],
            plane_send.at[a, p, k], plane_recv.at[a, p, k], ahead(k),
        )

    def a_copy(s):
        other = pl.ds(pl.multiple_of((1 - low) * half, 128), half)
        return copy(part.at[s, :, other], first_in.at[s], a_send.at[s], a_recv.at[s], near)

    def b_copy(s):
        other = pl.ds(pl.multiple_of((1 - high) * quarter, 128), quarter)
        return copy(first.at[s, :, other], second_in.at[s], b_send.at[s], b_recv.at[s], far)

    own_quarter = pl.ds(pl.multiple_of(low * half + high * quarter, 128), quarter)
    own_half = pl.ds(pl.multiple_of(low * half, 128), half)

    def c_copy(s):
        block = hidden.at[s, :, own_quarter]
        return copy(block, block, c_send.at[s], c_recv.at[s], far)

    def d_copy(s):
        block = hidden.at[s, :, own_half]
        return copy(block, block, d_send.at[s], d_recv.at[s], near)

    def dx_copy(k, p):
        return copy(
            dx.at[k, :, inner(p)], dx_in.at[k, :, inner(p)],
            dx_send.at[p, k], dx_recv.at[p, k], behind(k),
        )

    def cover_start(replica_index):
        return jnp.minimum(replica_index * own_rows // 128 * 128, width - cover)

    def y_copy(a, k):
        block = pl.ds(pl.multiple_of(cover_start((rep + 1) % n_rep), 128), cover)
        return copy(
            rows.at[a, k, :, block], rows_peer.at[a, k], y_send.at[a, k], y_recv.at[a, k], replica(1)
        )

    def h_copy(t):
        return copy(
            hidden.at[t, :, own_quarter], hidden_peer.at[t, :, own_quarter],
            h_send.at[t], h_recv.at[t], replica(1),
        )

    def f_copy(t):
        block = hidden_peer.at[t, :, own_quarter]
        return copy(block, block, f_send.at[t], f_recv.at[t], far)

    def g_copy(t):
        block = hidden_peer.at[t, :, own_half]
        return copy(block, block, g_send.at[t], g_recv.at[t], near)

    def gate_copy(k):
        return copy(gate_row.at[k], gate_in.at[k], gate_send.at[k], gate_recv.at[k], behind(k))

    def term_copy(a, d):
        return copy(
            terms.at[a, weight_rows((rep + d) % n_rep)], (up_sums, down_sums)[a].at[d],
            term_send.at[a, d], term_recv.at[a, d], replica(d),
        )

    def back_copy(j, p):
        return copy(
            back.at[(q + j) % SLICES, :, inner(p)], grad_tokens.at[:, feature_part(q, p)],
            back_send.at[p, j], back_recv.at[p, j], mate(j),
        )

    def mate_copy(j):
        return copy(gate_back.at[(q + j) % SLICES], gate_mates.at[j], mate_send.at[j], mate_recv.at[j], mate(j))

    def term_local(a):
        kept = weight_rows(rep)
        if pair:
            kept = pl.ds(pl.multiple_of(rep * own_rows - cover_start(rep), 16), own_rows)
        return pltpu.make_async_copy(
            terms.at[a, kept], (up_sums, down_sums)[a].at[0], local_sem.at[a]
        )

    cot_local = pltpu.make_async_copy(cot, cot_block, local_sem.at[4])
    cot_local.start()
    barrier = pltpu.get_barrier_semaphore()
    peers = [mate(j) for j in range(1, SLICES)] + [replica(d) for d in range(1, n_rep)]
    for device in peers:
        pl.semaphore_signal(barrier, inc=1, device_id=device, device_id_type=MESH)

    @pl.loop(1, planes)
    def _(k):
        pl.semaphore_signal(barrier, inc=1, device_id=ahead(k), device_id_type=MESH)

    pl.semaphore_wait(barrier, len(peers) + planes - 1)

    for j in range(1, SLICES):
        raw_copy(0, j, 0).start()
    for d in range(1, n_rep):
        weight_copy(0, d).start()
    local = [
        pltpu.make_async_copy(tokens.at[:, feature_block(q)], raw.at[0, q], local_sem.at[0]),
        pltpu.make_async_copy(w_up, weights.at[0, weight_rows(rep)], local_sem.at[1]),
        pltpu.make_async_copy(w_down, weights.at[1, weight_rows(rep)], local_sem.at[2]),
    ]
    for c in local:
        c.start()

    route = routes[...]
    count = max(8, planes)
    onehot = (lax.broadcasted_iota(jnp.int32, (count, tok_dev), 0) == route).astype(F32)
    before = (
        lax.broadcasted_iota(jnp.int32, (tok_dev, tok_dev), 0)
        < lax.broadcasted_iota(jnp.int32, (tok_dev, tok_dev), 1)
    ).astype(F32)
    slot = jnp.sum(onehot * dot(onehot, before, (1, 0)), axis=0, keepdims=True)
    position = (route * slots + q * capacity).astype(F32) + slot
    place[q] = jnp.broadcast_to(position, (8, tok_dev))
    for j in range(1, SLICES):
        place_copy(j).start()
    for p in range(1, len(parts)):
        for j in range(1, SLICES):
            raw_copy(0, j, p).start()

    square = lax.broadcasted_iota(jnp.int32, (tok_dev, tok_dev), 0) == lax.broadcasted_iota(
        jnp.int32, (tok_dev, tok_dev), 1
    )
    gate = jnp.sum(jnp.where(square, gates[...], 0.0), axis=1, keepdims=True)
    cot_local.wait()
    for m in range(SLICES):
        block = slice(m * width, (m + 1) * width)
        out_grad[:, block] = (gate * cot_block[:, block].astype(F32)).astype(BF16)
    local_grad = pltpu.make_async_copy(
        out_grad.at[:, feature_block(q)], raw.at[1, q], local_sem.at[3]
    )
    local_grad.start()
    gate_row[...] = jnp.zeros_like(gate_row)

    for j in range(1, SLICES):
        place_copy(j).wait_recv()
    places = jnp.concatenate([place[m, 0:1, :] for m in range(SLICES)], axis=1)

    @pl.loop(0, planes)
    def _(k):
        number = lax.broadcasted_iota(jnp.int32, (slots, SLICES * tok_dev), 0)
        number = (number + (plane + k) % planes * slots).astype(F32)
        matrix[k] = jnp.where(number == places, 1.0, 0.0).astype(BF16)

    def pack(a, k, p, target):
        begin, length = parts[p]
        for start, size in tiles(length):
            block = slice(begin + start, begin + start + size)
            source = raw[a, :, :, block].reshape(SLICES * tok_dev, size)
            target[a, k, :, block] = dot(matrix[k], source, (1, 0)).astype(BF16)

    for a in range(2):
        (local[0], local_grad)[a].wait()
        for p in range(len(parts)):
            for j in range(1, SLICES):
                landed = raw.at[a, (q + SLICES - j) % SLICES, :, inner(p)]
                copy(
                    landed, landed, raw_send.at[a, p, j], raw_recv.at[a, p, j], mate(j)
                ).wait_recv()
            if a == 0:
                for j in range(1, SLICES):
                    raw_copy(1, j, p).start()

            @pl.loop(1, planes)
            def _(k):
                pack(a, k, p, packed)

                @pl.when(k < hops)
                def _():
                    plane_copy(a, k, p).start()

            pack(a, 0, p, rows)
        if pair:
            y_copy(a, 0).start()
    local[1].wait()
    local[2].wait()

    def dx_product(k, p, target):
        left = hidden[planes + k]
        begin, length = parts[p]
        for start, size in tiles(length):
            block = slice(begin + start, begin + start + size)
            target[k, :, block] = dot(left, weights[0, block, :], (1, 1)).astype(BF16)

    def split(value):
        upper = value.astype(BF16)
        return upper, (value - upper.astype(F32)).astype(BF16)

    def weight_term(a):
        right = hidden[(1 - a) * planes : (2 - a) * planes].reshape(planes * slots, hid)
        for start, size in tiles(width, 512):
            left = rows[a, :, :, start : start + size].reshape(planes * slots, size)
            terms[a, start : start + size, :] = dot(left, right, (0, 0)).astype(BF16)
        for d in range(1, n_rep):
            term_copy(a, d).start()
        term_local(a).start()

    def pair_term(a):
        @pl.loop((1 - a) * planes, (2 - a) * planes)
        def _(t):
            landed = hidden_peer.at[t, :, pl.ds(pl.multiple_of((1 - low) * half, 128), half)]
            copy(landed, landed, g_send.at[t], g_recv.at[t], near).wait_recv()

        @pl.loop(0, planes)
        def _(k):
            landed = rows_peer.at[a, k]
            copy(landed, landed, y_send.at[a, k], y_recv.at[a, k], replica(1)).wait_recv()

        count = planes * slots
        mine = pl.ds(pl.multiple_of(cover_start(rep), 128), cover)
        some = slice((1 - a) * planes, (2 - a) * planes)
        total = dot(
            rows[a, :, :, mine].reshape(count, cover), hidden[some].reshape(count, hid), (0, 0)
        )
        total += dot(
            rows_peer[a].reshape(count, cover), hidden_peer[some].reshape(count, hid), (0, 0)
        )
        terms[a] = total.astype(BF16)
        term_local(a).start()

    @pl.loop(0, last_slot + (7 if pair else 5))
    def _(s):
        def stage(lag):
            slot = s - lag
            item = jnp.where(slot < hops, slot, slot + 1)
            item = jnp.where(slot < early, item, (slot - early - 3) * planes - 1)
            here = (slot >= 0) & (slot <= last_slot)
            return item, here & ((slot < early) | (slot >= early + 4))

        e_item, e_here = stage(4)

        @pl.when(e_here)
        def _():
            t = e_item
            landed = hidden.at[t, :, pl.ds(pl.multiple_of((1 - low) * half, 128), half)]
            copy(landed, landed, d_send.at[t], d_recv.at[t], near).wait_recv()

            @pl.when(t >= planes)
            def _():
                k = t - planes
                @pl.when(k == 0)
                def _():
                    for p in range(len(parts)):
                        dx_product(0, p, dx_in)

                @pl.when(k > 0)
                def _():
                    gate_copy(k).start()
                    for p in range(len(parts)):
                        dx_product(k, p, dx)
                        dx_copy(k, p).start()

        d_item, d_here = stage(3)

        @pl.when(d_here)
        def _():
            t = d_item
            landed = hidden.at[
                t, :, pl.ds(pl.multiple_of(low * half + (1 - high) * quarter, 128), quarter)
            ]
            copy(landed, landed, c_send.at[t], c_recv.at[t], far).wait_recv()
            d_copy(t).start()

        c_item, c_here = stage(2)

        @pl.when(c_here)
        def _():
            t = c_item
            b_copy(t).wait_recv()
            mine = pl.ds(pl.multiple_of(high * quarter, 128), quarter)
            total = first[t, :, mine].astype(F32) + second_in[t].astype(F32)

            @pl.when(t < planes)
            def _():
                act[t] = total
                hidden[t, :, own_quarter] = (total * jax.nn.sigmoid(total)).astype(BF16)

            @pl.when(t >= planes)
            def _():
                k = t - planes
                value = act[k]
                gating = jax.nn.sigmoid(value)
                hidden[t, :, own_quarter] = (
                    total * gating * (1.0 + value * (1.0 - gating))
                ).astype(BF16)
                upper, lower = split(total * (value * gating))
                ones = jnp.ones((16, quarter), BF16)
                sums = dot(ones, upper, (1, 1)) + dot(ones, lower, (1, 1))
                gate_row[k, :, 0:slots] = sums[0:8]

            c_copy(t).start()
            if pair:
                h_copy(t).start()

        b_item, b_here = stage(1)

        @pl.when(b_here)
        def _():
            t = b_item
            a_copy(t).wait_recv()
            first[t] = (part[t, :, own_half].astype(F32) + first_in[t].astype(F32)).astype(BF16)
            b_copy(t).start()

        i, here = stage(0)

        @pl.when(here)
        def _():
            a, k = i // planes, i % planes

            @pl.when(k == 0)
            def _():
                for d in range(1, n_rep):
                    landed = weights.at[a, weight_rows((rep + n_rep - d) % n_rep)]
                    copy(
                        landed, landed, weight_send.at[a, d], weight_recv.at[a, d], replica(d)
                    ).wait_recv()

                @pl.when(a == 0)
                def _():
                    for d in range(1, n_rep):
                        weight_copy(1, d).start()

            @pl.when(k > 0)
            def _():
                for p in range(len(parts)):
                    plane_copy(a, k, p).wait_recv()
                if pair:
                    y_copy(a, k).start()

            @pl.when(i == items - 3)
            def _():
                for b in range(2):
                    for p in range(len(parts)):
                        plane_copy(b, hops, p).start()

            left = rows[a, k]
            for start, size in tiles(hid):
                part[i, :, start : start + size] = dot(
                    left, weights[a, :, start : start + size], (1, 0)
                ).astype(BF16)
            a_copy(i).start()

        if pair:
            f_item, f_here = stage(5)

            @pl.when(f_here)
            def _():
                h_copy(f_item).wait_recv()
                f_copy(f_item).start()

            g_item, g_here = stage(6)

            @pl.when(g_here)
            def _():
                t = g_item
                landed = hidden_peer.at[
                    t, :, pl.ds(pl.multiple_of(low * half + (1 - high) * quarter, 128), quarter)
                ]
                copy(landed, landed, f_send.at[t], f_recv.at[t], far).wait_recv()
                g_copy(t).start()

            @pl.when(s == last_slot + 5)
            def _():
                pair_term(1)
        else:
            @pl.when(s == last_slot + 3)
            def _():
                weight_term(1)

    (pair_term if pair else weight_term)(0)

    @pl.loop(1, planes)
    def _(k):
        gate_copy(k).wait_recv()

    for p in range(len(parts)):
        @pl.loop(1, planes)
        def _(k):
            dx_copy(k, p).wait_recv()

        every = matrix[...].reshape(planes * slots, SLICES * tok_dev)
        landed = dx_in[:, :, inner(p)].reshape(planes * slots, parts[p][1])
        token_rows = dot(every, landed, (0, 0)).astype(BF16)
        back[:, :, inner(p)] = token_rows.reshape(SLICES, tok_dev, parts[p][1])
        for j in (2, 1, 3):
            back_copy(j, p).start()
        if p == 0:
            sums = jnp.zeros((8, SLICES * tok_dev), F32)
            for k in range(planes):
                upper, lower = split((gate_row if k == 0 else gate_in)[k, :, 0:slots])
                both = dot(jnp.concatenate([upper, lower], axis=0), matrix[k], (1, 0))
                sums += both[0:8] + both[8:16]
            for m in range(SLICES):
                gate_back[m] = sums[:, m * tok_dev : (m + 1) * tok_dev]
            for j in range(1, SLICES):
                mate_copy(j).start()
    last = pltpu.make_async_copy(
        back.at[q], grad_tokens.at[:, feature_block(q)], local_sem.at[2]
    )
    last.start()
    total = gate_back[q]
    for j in range(1, SLICES):
        mate_copy(j).wait_recv()
        total += gate_mates[j]
    gate_sums[...] = total[0:1] / gates[...]
    last.wait()
    for p in range(len(parts)):
        for j in range(1, SLICES):
            landed = grad_tokens.at[:, feature_part((q + SLICES - j) % SLICES, p)]
            copy(landed, landed, back_send.at[p, j], back_recv.at[p, j], mate(j)).wait_recv()
            back_copy(j, p).wait_send()
    for a in range(2):
        term_local(a).wait()
        for d in range(1, n_rep):
            if not pair:
                term_copy(a, d).wait_recv()
                term_copy(a, d).wait_send()
            weight_copy(a, d).wait_send()
        for j in range(1, SLICES):
            for p in range(len(parts)):
                raw_copy(a, j, p).wait_send()

        @pl.loop(1, planes)
        def _(k):
            for p in range(len(parts)):
                plane_copy(a, k, p).wait_send()

    for j in range(1, SLICES):
        place_copy(j).wait_send()
        mate_copy(j).wait_send()

    @pl.loop(1, planes)
    def _(k):
        for p in range(len(parts)):
            dx_copy(k, p).wait_send()
        gate_copy(k).wait_send()

    @pl.loop(0, items)
    def _(s):
        a_copy(s).wait_send()
        b_copy(s).wait_send()
        c_copy(s).wait_send()
        d_copy(s).wait_send()
        if pair:
            h_copy(s).wait_send()
            f_copy(s).wait_send()
            g_copy(s).wait_send()
            y_copy(s // planes, s % planes).wait_send()


def shards(tokens, cotangent, gates, routes, w_up, w_down_t):
    tok_dev, top_count = routes.shape
    model_width = tokens.shape[1]
    width = model_width // SLICES
    n_rep, n_exp = lax.axis_size("rep"), lax.axis_size("exp")
    planes = n_exp // SLICES
    capacity = min(tok_dev, max(2, 9 * tok_dev * top_count // (8 * planes)))
    slots = -(-SLICES * capacity // 16) * 16
    lanes = -(-slots // 128) * 128
    own_rows, hid = w_up.shape
    items = 2 * planes
    pair = n_rep == 2
    cover = max(
        -(-(r + 1) * own_rows // 128) * 128 - r * own_rows // 128 * 128 for r in range(n_rep)
    )
    sums = 1 if pair else n_rep
    peer = planes if pair else 1
    n_parts = len(tiles(width, 512))
    dma = pltpu.SemaphoreType.DMA
    vmem = pl.BlockSpec(memory_space=pltpu.VMEM)
    hbm = pl.BlockSpec(memory_space=pl.ANY)
    pairs = []
    for shape in (
        (2, n_parts, SLICES), (SLICES,), (2, n_rep), (2, n_parts, planes), (items,), (items,), (items,), (items,),
        (n_parts, planes), (planes,), (2, n_rep), (n_parts, SLICES), (SLICES,),
        (2, planes), (items,), (items,), (items,),
    ):
        pairs += [dma(shape), dma(shape)]
    grad_tokens, gate_sums, up_sums, down_sums = pl.pallas_call(
        functools.partial(kernel, n_rep, planes, capacity, slots, pair, cover),
        out_shape=(
            jax.ShapeDtypeStruct((tok_dev, model_width), BF16),
            jax.ShapeDtypeStruct((1, tok_dev), F32),
            jax.ShapeDtypeStruct((sums, own_rows, hid), BF16),
            jax.ShapeDtypeStruct((sums, own_rows, hid), BF16),
        ),
        in_specs=[hbm, hbm, vmem, vmem, hbm, hbm],
        out_specs=(hbm, vmem, hbm, hbm),
        scratch_shapes=[
            pltpu.VMEM((tok_dev, model_width), BF16),
            pltpu.VMEM((tok_dev, model_width), BF16),
            pltpu.VMEM((2, SLICES, tok_dev, width), BF16),
            pltpu.VMEM((SLICES, 8, tok_dev), F32),
            pltpu.VMEM((2, width, hid), BF16),
            pltpu.VMEM((2, planes, slots, width), BF16),
            pltpu.VMEM((2, planes, slots, width), BF16),
            pltpu.VMEM((items, slots, hid), BF16),
            pltpu.VMEM((items, slots, hid // 2), BF16),
            pltpu.VMEM((items, slots, hid // 2), BF16),
            pltpu.VMEM((items, slots, hid // 4), BF16),
            pltpu.VMEM((planes, slots, hid // 4), F32),
            pltpu.VMEM((items, slots, hid), BF16),
            pltpu.VMEM((2, cover if pair else width, hid), BF16),
            pltpu.VMEM((planes, slots, width), BF16),
            pltpu.VMEM((planes, slots, width), BF16),
            pltpu.VMEM((planes, 8, lanes), F32),
            pltpu.VMEM((planes, 8, lanes), F32),
            pltpu.VMEM((SLICES, tok_dev, width), BF16),
            pltpu.VMEM((SLICES, 8, tok_dev), F32),
            pltpu.VMEM((SLICES, 8, tok_dev), F32),
            pltpu.VMEM((2, peer, slots, cover), BF16),
            pltpu.VMEM((2 * peer, slots, hid), BF16),
            pltpu.VMEM((planes, slots, SLICES * tok_dev), BF16),
            dma((5,)),
            *pairs,
        ],
        compiler_params=pltpu.CompilerParams(
            collective_id=0, has_side_effects=True, vmem_limit_bytes=56 * 1024 * 1024
        ),
        cost_estimate=pl.CostEstimate(
            flops=12 * planes * slots * width * hid, bytes_accessed=8 * 1024 * 1024, transcendentals=0
        ),
    )(tokens, cotangent, gates.reshape(1, tok_dev), routes.reshape(1, tok_dev), w_up, w_down_t)
    grad_up = sum(up_sums[d].astype(F32) for d in range(sums))
    grad_down_t = sum(down_sums[d].astype(F32) for d in range(sums))
    return grad_tokens, gate_sums.reshape(tok_dev, top_count), grad_up, grad_down_t


def solution(mesh):
    split = P(("rep", "exp"), None)
    weight_split = P(("exp", "rep"), None)
    return jax.shard_map(
        shards,
        mesh=mesh,
        in_specs=(split, split, split, split, weight_split, weight_split),
        out_specs=(split, split, weight_split, weight_split),
        check_vma=False,
    )
```

```python
import functools

import jax
import jax.numpy as jnp
from jax import lax
from jax.experimental import pallas as pl
from jax.experimental.pallas import tpu as pltpu
from jax.sharding import PartitionSpec as P

SLICES = 4
MESH = pl.DeviceIdType.MESH
F32, BF16 = jnp.float32, jnp.bfloat16


def dot(left, right, dims, precision=None):
    return lax.dot_general(
        left, right, ((dims[:1], dims[1:]), ((), ())), preferred_element_type=F32, precision=precision
    )


def tiles(width, step=256):
    return [(start, min(step, width - start)) for start in range(0, width, step)]


def kernel(
    n_rep, planes, capacity, slots, pair, cover,
    tokens, cot, gates, routes, w_up, w_down,
    grad_tokens, gate_sums, up_sums, down_sums,
    cot_block, out_grad, raw, place, weights, packed, rows, part, first, first_in, second_in,
    act, hidden, terms, dx, dx_in, gate_row, gate_in, back, gate_back, gate_mates,
    rows_peer, hidden_peer, matrix,
    local_sem, raw_send, raw_recv, place_send, place_recv, weight_send, weight_recv,
    plane_send, plane_recv, a_send, a_recv, b_send, b_recv, c_send, c_recv, d_send, d_recv,
    dx_send, dx_recv, gate_send, gate_recv, term_send, term_recv, back_send, back_recv,
    mate_send, mate_recv, y_send, y_recv, h_send, h_recv, f_send, f_recv, g_send, g_recv,
):
    rep, me = lax.axis_index("rep"), lax.axis_index("exp")
    plane, q = me // SLICES, me % SLICES
    low, high = q % 2, q // 2
    tok_dev, width = raw.shape[2], raw.shape[3]
    own_rows, hid = w_up.shape
    half, quarter = hid // 2, hid // 4
    items = 2 * planes
    parts = tiles(width, 512)
    last_slot = items - 1

    def mate(distance):
        return (rep, plane * SLICES + (q + distance) % SLICES)

    def ahead(distance):
        return (rep, (plane + distance) % planes * SLICES + q)

    def behind(distance):
        return (rep, (plane + planes - distance) % planes * SLICES + q)

    def replica(distance):
        return ((rep + distance) % n_rep, me)

    near = (rep, plane * SLICES + high * 2 + 1 - low)
    far = (rep, plane * SLICES + (1 - high) * 2 + low)

    def copy(source, target, send_sem, recv_sem, device):
        return pltpu.make_async_remote_copy(
            src_ref=source, dst_ref=target, send_sem=send_sem, recv_sem=recv_sem,
            device_id=device, device_id_type=MESH,
        )

    def feature_block(index):
        return pl.ds(pl.multiple_of(index * width, 128), width)

    def weight_rows(index):
        return pl.ds(pl.multiple_of(index * own_rows, 16), own_rows)

    def feature_part(index, p):
        start, size = parts[p]
        return pl.ds(pl.multiple_of(index * width + start, 128), size)

    def inner(p):
        start, size = parts[p]
        return slice(start, start + size)

    def raw_copy(a, j, p):
        source = (tokens, out_grad)[a]
        return copy(
            source.at[:, feature_part((q + j) % SLICES, p)], raw.at[a, q, :, inner(p)],
            raw_send.at[a, p, j], raw_recv.at[a, p, j], mate(j),
        )

    def place_copy(j):
        return copy(place.at[q], place.at[q], place_send.at[j], place_recv.at[j], mate(j))

    def weight_copy(a, d):
        source = (w_up, w_down)[a]
        return copy(
            source, weights.at[a, weight_rows(rep)],
            weight_send.at[a, d], weight_recv.at[a, d], replica(d),
        )

    def plane_copy(a, k, p):
        return copy(
            packed.at[a, k, :, inner(p)], rows.at[a, k, :, inner(p)],
            plane_send.at[a, p, k], plane_recv.at[a, p, k], ahead(k),
        )

    def a_copy(s):
        other = pl.ds(pl.multiple_of((1 - low) * half, 128), half)
        return copy(part.at[s, :, other], first_in.at[s], a_send.at[s], a_recv.at[s], near)

    def b_copy(s):
        other = pl.ds(pl.multiple_of((1 - high) * quarter, 128), quarter)
        return copy(first.at[s, :, other], second_in.at[s], b_send.at[s], b_recv.at[s], far)

    own_quarter = pl.ds(pl.multiple_of(low * half + high * quarter, 128), quarter)
    own_half = pl.ds(pl.multiple_of(low * half, 128), half)

    def c_copy(s):
        block = hidden.at[s, :, own_quarter]
        return copy(block, block, c_send.at[s], c_recv.at[s], far)

    def d_copy(s):
        block = hidden.at[s, :, own_half]
        return copy(block, block, d_send.at[s], d_recv.at[s], near)

    def dx_copy(k, p):
        return copy(
            dx.at[k, :, inner(p)], dx_in.at[k, :, inner(p)],
            dx_send.at[p, k], dx_recv.at[p, k], behind(k),
        )

    def cover_start(replica_index):
        return jnp.minimum(replica_index * own_rows // 128 * 128, width - cover)

    def y_copy(a, k):
        block = pl.ds(pl.multiple_of(cover_start((rep + 1) % n_rep), 128), cover)
        return copy(
            rows.at[a, k, :, block], rows_peer.at[a, k], y_send.at[a, k], y_recv.at[a, k], replica(1)
        )

    def h_copy(t):
        return copy(
            hidden.at[t, :, own_quarter], hidden_peer.at[t, :, own_quarter],
            h_send.at[t], h_recv.at[t], replica(1),
        )

    def f_copy(t):
        block = hidden_peer.at[t, :, own_quarter]
        return copy(block, block, f_send.at[t], f_recv.at[t], far)

    def g_copy(t):
        block = hidden_peer.at[t, :, own_half]
        return copy(block, block, g_send.at[t], g_recv.at[t], near)

    def gate_copy(k):
        return copy(gate_row.at[k], gate_in.at[k], gate_send.at[k], gate_recv.at[k], behind(k))

    def term_copy(a, d):
        return copy(
            terms.at[a, weight_rows((rep + d) % n_rep)], (up_sums, down_sums)[a].at[d],
            term_send.at[a, d], term_recv.at[a, d], replica(d),
        )

    def back_copy(j, p):
        return copy(
            back.at[(q + j) % SLICES, :, inner(p)], grad_tokens.at[:, feature_part(q, p)],
            back_send.at[p, j], back_recv.at[p, j], mate(j),
        )

    def mate_copy(j):
        return copy(gate_back.at[(q + j) % SLICES], gate_mates.at[j], mate_send.at[j], mate_recv.at[j], mate(j))

    def term_local(a):
        kept = weight_rows(rep)
        if pair:
            kept = pl.ds(pl.multiple_of(rep * own_rows - cover_start(rep), 16), own_rows)
        return pltpu.make_async_copy(
            terms.at[a, kept], (up_sums, down_sums)[a].at[0], local_sem.at[a]
        )

    cot_local = pltpu.make_async_copy(cot, cot_block, local_sem.at[4])
    cot_local.start()
    barrier = pltpu.get_barrier_semaphore()
    peers = [mate(j) for j in range(1, SLICES)] + [replica(d) for d in range(1, n_rep)]
    for device in peers:
        pl.semaphore_signal(barrier, inc=1, device_id=device, device_id_type=MESH)

    @pl.loop(1, planes)
    def _(k):
        pl.semaphore_signal(barrier, inc=1, device_id=ahead(k), device_id_type=MESH)

    pl.semaphore_wait(barrier, len(peers) + planes - 1)

    for j in range(1, SLICES):
        raw_copy(0, j, 0).start()
    for d in range(1, n_rep):
        weight_copy(0, d).start()
    local = [
        pltpu.make_async_copy(tokens.at[:, feature_block(q)], raw.at[0, q], local_sem.at[0]),
        pltpu.make_async_copy(w_up, weights.at[0, weight_rows(rep)], local_sem.at[1]),
        pltpu.make_async_copy(w_down, weights.at[1, weight_rows(rep)], local_sem.at[2]),
    ]
    for c in local:
        c.start()

    route = routes[...]
    count = max(8, planes)
    onehot = (lax.broadcasted_iota(jnp.int32, (count, tok_dev), 0) == route).astype(F32)
    before = (
        lax.broadcasted_iota(jnp.int32, (tok_dev, tok_dev), 0)
        < lax.broadcasted_iota(jnp.int32, (tok_dev, tok_dev), 1)
    ).astype(F32)
    slot = jnp.sum(onehot * dot(onehot, before, (1, 0)), axis=0, keepdims=True)
    position = (route * slots + q * capacity).astype(F32) + slot
    place[q] = jnp.broadcast_to(position, (8, tok_dev))
    for j in range(1, SLICES):
        place_copy(j).start()
    for p in range(1, len(parts)):
        for j in range(1, SLICES):
            raw_copy(0, j, p).start()

    square = lax.broadcasted_iota(jnp.int32, (tok_dev, tok_dev), 0) == lax.broadcasted_iota(
        jnp.int32, (tok_dev, tok_dev), 1
    )
    gate = jnp.sum(jnp.where(square, gates[...], 0.0), axis=1, keepdims=True)
    cot_local.wait()
    for m in range(SLICES):
        block = slice(m * width, (m + 1) * width)
        out_grad[:, block] = (gate * cot_block[:, block].astype(F32)).astype(BF16)
    local_grad = pltpu.make_async_copy(
        out_grad.at[:, feature_block(q)], raw.at[1, q], local_sem.at[3]
    )
    local_grad.start()
    gate_row[...] = jnp.zeros_like(gate_row)

    for j in range(1, SLICES):
        place_copy(j).wait_recv()
    places = jnp.concatenate([place[m, 0:1, :] for m in range(SLICES)], axis=1)

    @pl.loop(0, planes)
    def _(k):
        number = lax.broadcasted_iota(jnp.int32, (slots, SLICES * tok_dev), 0)
        number = (number + (plane + k) % planes * slots).astype(F32)
        matrix[k] = jnp.where(number == places, 1.0, 0.0).astype(BF16)

    def pack(a, k, p, target):
        begin, length = parts[p]
        for start, size in tiles(length):
            block = slice(begin + start, begin + start + size)
            source = raw[a, :, :, block].reshape(SLICES * tok_dev, size)
            target[a, k, :, block] = dot(matrix[k], source, (1, 0)).astype(BF16)

    for a in range(2):
        (local[0], local_grad)[a].wait()
        for p in range(len(parts)):
            for j in range(1, SLICES):
                landed = raw.at[a, (q + SLICES - j) % SLICES, :, inner(p)]
                copy(
                    landed, landed, raw_send.at[a, p, j], raw_recv.at[a, p, j], mate(j)
                ).wait_recv()
            if a == 0:
                for j in range(1, SLICES):
                    raw_copy(1, j, p).start()

            @pl.loop(1, planes)
            def _(k):
                pack(a, k, p, packed)
                plane_copy(a, k, p).start()

            pack(a, 0, p, rows)
        if pair:
            y_copy(a, 0).start()
    local[1].wait()
    local[2].wait()

    def dx_product(k, p, target):
        left = hidden[planes + k]
        begin, length = parts[p]
        for start, size in tiles(length):
            block = slice(begin + start, begin + start + size)
            target[k, :, block] = dot(left, weights[0, block, :], (1, 1)).astype(BF16)

    def split(value):
        upper = value.astype(BF16)
        return upper, (value - upper.astype(F32)).astype(BF16)

    def weight_term(a):
        right = hidden[(1 - a) * planes : (2 - a) * planes].reshape(planes * slots, hid)
        for start, size in tiles(width, 512):
            left = rows[a, :, :, start : start + size].reshape(planes * slots, size)
            terms[a, start : start + size, :] = dot(left, right, (0, 0)).astype(BF16)
        for d in range(1, n_rep):
            term_copy(a, d).start()
        term_local(a).start()

    def pair_term(a):
        @pl.loop((1 - a) * planes, (2 - a) * planes)
        def _(t):
            landed = hidden_peer.at[t, :, pl.ds(pl.multiple_of((1 - low) * half, 128), half)]
            copy(landed, landed, g_send.at[t], g_recv.at[t], near).wait_recv()

        @pl.loop(0, planes)
        def _(k):
            landed = rows_peer.at[a, k]
            copy(landed, landed, y_send.at[a, k], y_recv.at[a, k], replica(1)).wait_recv()

        count = planes * slots
        mine = pl.ds(pl.multiple_of(cover_start(rep), 128), cover)
        some = slice((1 - a) * planes, (2 - a) * planes)
        total = dot(
            rows[a, :, :, mine].reshape(count, cover), hidden[some].reshape(count, hid), (0, 0)
        )
        total += dot(
            rows_peer[a].reshape(count, cover), hidden_peer[some].reshape(count, hid), (0, 0)
        )
        terms[a] = total.astype(BF16)
        term_local(a).start()

    @pl.loop(0, last_slot + (7 if pair else 6))
    def _(s):
        def stage(lag):
            return s - lag, (s >= lag) & (s <= last_slot + lag)

        e_item, e_here = stage(4)

        @pl.when(e_here)
        def _():
            t = e_item
            landed = hidden.at[t, :, pl.ds(pl.multiple_of((1 - low) * half, 128), half)]
            copy(landed, landed, d_send.at[t], d_recv.at[t], near).wait_recv()

            @pl.when(t >= planes)
            def _():
                k = t - planes
                @pl.when(k == 0)
                def _():
                    for p in range(len(parts)):
                        dx_product(0, p, dx_in)

                @pl.when(k > 0)
                def _():
                    dx_product(k, 0, dx)
                    dx_copy(k, 0).start()
                    gate_copy(k).start()

        d_item, d_here = stage(3)

        @pl.when(d_here)
        def _():
            t = d_item
            landed = hidden.at[
                t, :, pl.ds(pl.multiple_of(low * half + (1 - high) * quarter, 128), quarter)
            ]
            copy(landed, landed, c_send.at[t], c_recv.at[t], far).wait_recv()
            d_copy(t).start()

        c_item, c_here = stage(2)

        @pl.when(c_here)
        def _():
            t = c_item
            b_copy(t).wait_recv()
            mine = pl.ds(pl.multiple_of(high * quarter, 128), quarter)
            total = first[t, :, mine].astype(F32) + second_in[t].astype(F32)

            @pl.when(t < planes)
            def _():
                act[t] = total
                hidden[t, :, own_quarter] = (total * jax.nn.sigmoid(total)).astype(BF16)

            @pl.when(t >= planes)
            def _():
                k = t - planes
                value = act[k]
                gating = jax.nn.sigmoid(value)
                hidden[t, :, own_quarter] = (
                    total * gating * (1.0 + value * (1.0 - gating))
                ).astype(BF16)
                upper, lower = split(total * (value * gating))
                ones = jnp.ones((16, quarter), BF16)
                sums = dot(ones, upper, (1, 1)) + dot(ones, lower, (1, 1))
                gate_row[k, :, 0:slots] = sums[0:8]

            c_copy(t).start()
            if pair:
                h_copy(t).start()

        b_item, b_here = stage(1)

        @pl.when(b_here)
        def _():
            t = b_item
            a_copy(t).wait_recv()
            first[t] = (part[t, :, own_half].astype(F32) + first_in[t].astype(F32)).astype(BF16)
            b_copy(t).start()

        i, here = stage(0)

        @pl.when(here)
        def _():
            a, k = i // planes, i % planes

            @pl.when(k == 0)
            def _():
                for d in range(1, n_rep):
                    landed = weights.at[a, weight_rows((rep + n_rep - d) % n_rep)]
                    copy(
                        landed, landed, weight_send.at[a, d], weight_recv.at[a, d], replica(d)
                    ).wait_recv()

                @pl.when(a == 0)
                def _():
                    for d in range(1, n_rep):
                        weight_copy(1, d).start()

            @pl.when(k > 0)
            def _():
                for p in range(len(parts)):
                    plane_copy(a, k, p).wait_recv()
                if pair:
                    y_copy(a, k).start()

            left = rows[a, k]
            for start, size in tiles(hid):
                part[i, :, start : start + size] = dot(
                    left, weights[a, :, start : start + size], (1, 0)
                ).astype(BF16)
            a_copy(i).start()

        @pl.when(s == last_slot + 5)
        def _():
            for p in range(1, len(parts)):
                @pl.loop(1, planes)
                def _(k):
                    dx_product(k, p, dx)
                    dx_copy(k, p).start()

        if pair:
            f_item, f_here = stage(5)

            @pl.when(f_here)
            def _():
                h_copy(f_item).wait_recv()
                f_copy(f_item).start()

            g_item, g_here = stage(6)

            @pl.when(g_here)
            def _():
                t = g_item
                landed = hidden_peer.at[
                    t, :, pl.ds(pl.multiple_of(low * half + (1 - high) * quarter, 128), quarter)
                ]
                copy(landed, landed, f_send.at[t], f_recv.at[t], far).wait_recv()
                g_copy(t).start()

            @pl.when(s == last_slot + 6)
            def _():
                pair_term(1)
        else:
            @pl.when(s == last_slot + 3)
            def _():
                weight_term(1)

    (pair_term if pair else weight_term)(0)

    @pl.loop(1, planes)
    def _(k):
        gate_copy(k).wait_recv()

    for p in range(len(parts)):
        @pl.loop(1, planes)
        def _(k):
            dx_copy(k, p).wait_recv()

        every = matrix[...].reshape(planes * slots, SLICES * tok_dev)
        landed = dx_in[:, :, inner(p)].reshape(planes * slots, parts[p][1])
        token_rows = dot(every, landed, (0, 0)).astype(BF16)
        back[:, :, inner(p)] = token_rows.reshape(SLICES, tok_dev, parts[p][1])
        for j in (2, 1, 3):
            back_copy(j, p).start()
        if p == 0:
            sums = jnp.zeros((8, SLICES * tok_dev), F32)
            for k in range(planes):
                upper, lower = split((gate_row if k == 0 else gate_in)[k, :, 0:slots])
                both = dot(jnp.concatenate([upper, lower], axis=0), matrix[k], (1, 0))
                sums += both[0:8] + both[8:16]
            for m in range(SLICES):
                gate_back[m] = sums[:, m * tok_dev : (m + 1) * tok_dev]
            for j in range(1, SLICES):
                mate_copy(j).start()
    last = pltpu.make_async_copy(
        back.at[q], grad_tokens.at[:, feature_block(q)], local_sem.at[2]
    )
    last.start()
    total = gate_back[q]
    for j in range(1, SLICES):
        mate_copy(j).wait_recv()
        total += gate_mates[j]
    gate_sums[...] = total[0:1] / gates[...]
    last.wait()
    for p in range(len(parts)):
        for j in range(1, SLICES):
            landed = grad_tokens.at[:, feature_part((q + SLICES - j) % SLICES, p)]
            copy(landed, landed, back_send.at[p, j], back_recv.at[p, j], mate(j)).wait_recv()
            back_copy(j, p).wait_send()
    for a in range(2):
        term_local(a).wait()
        for d in range(1, n_rep):
            if not pair:
                term_copy(a, d).wait_recv()
                term_copy(a, d).wait_send()
            weight_copy(a, d).wait_send()
        for j in range(1, SLICES):
            for p in range(len(parts)):
                raw_copy(a, j, p).wait_send()

        @pl.loop(1, planes)
        def _(k):
            for p in range(len(parts)):
                plane_copy(a, k, p).wait_send()

    for j in range(1, SLICES):
        place_copy(j).wait_send()
        mate_copy(j).wait_send()

    @pl.loop(1, planes)
    def _(k):
        for p in range(len(parts)):
            dx_copy(k, p).wait_send()
        gate_copy(k).wait_send()

    @pl.loop(0, items)
    def _(s):
        a_copy(s).wait_send()
        b_copy(s).wait_send()
        c_copy(s).wait_send()
        d_copy(s).wait_send()
        if pair:
            h_copy(s).wait_send()
            f_copy(s).wait_send()
            g_copy(s).wait_send()
            y_copy(s // planes, s % planes).wait_send()


def shards(tokens, cotangent, gates, routes, w_up, w_down_t):
    tok_dev, top_count = routes.shape
    model_width = tokens.shape[1]
    width = model_width // SLICES
    n_rep, n_exp = lax.axis_size("rep"), lax.axis_size("exp")
    planes = n_exp // SLICES
    capacity = min(tok_dev, max(2, 9 * tok_dev * top_count // (8 * planes)))
    slots = -(-SLICES * capacity // 16) * 16
    lanes = -(-slots // 128) * 128
    own_rows, hid = w_up.shape
    items = 2 * planes
    pair = n_rep == 2
    cover = max(
        -(-(r + 1) * own_rows // 128) * 128 - r * own_rows // 128 * 128 for r in range(n_rep)
    )
    sums = 1 if pair else n_rep
    peer = planes if pair else 1
    n_parts = len(tiles(width, 512))
    dma = pltpu.SemaphoreType.DMA
    vmem = pl.BlockSpec(memory_space=pltpu.VMEM)
    hbm = pl.BlockSpec(memory_space=pl.ANY)
    pairs = []
    for shape in (
        (2, n_parts, SLICES), (SLICES,), (2, n_rep), (2, n_parts, planes), (items,), (items,), (items,), (items,),
        (n_parts, planes), (planes,), (2, n_rep), (n_parts, SLICES), (SLICES,),
        (2, planes), (items,), (items,), (items,),
    ):
        pairs += [dma(shape), dma(shape)]
    grad_tokens, gate_sums, up_sums, down_sums = pl.pallas_call(
        functools.partial(kernel, n_rep, planes, capacity, slots, pair, cover),
        out_shape=(
            jax.ShapeDtypeStruct((tok_dev, model_width), BF16),
            jax.ShapeDtypeStruct((1, tok_dev), F32),
            jax.ShapeDtypeStruct((sums, own_rows, hid), BF16),
            jax.ShapeDtypeStruct((sums, own_rows, hid), BF16),
        ),
        in_specs=[hbm, hbm, vmem, vmem, hbm, hbm],
        out_specs=(hbm, vmem, hbm, hbm),
        scratch_shapes=[
            pltpu.VMEM((tok_dev, model_width), BF16),
            pltpu.VMEM((tok_dev, model_width), BF16),
            pltpu.VMEM((2, SLICES, tok_dev, width), BF16),
            pltpu.VMEM((SLICES, 8, tok_dev), F32),
            pltpu.VMEM((2, width, hid), BF16),
            pltpu.VMEM((2, planes, slots, width), BF16),
            pltpu.VMEM((2, planes, slots, width), BF16),
            pltpu.VMEM((items, slots, hid), BF16),
            pltpu.VMEM((items, slots, hid // 2), BF16),
            pltpu.VMEM((items, slots, hid // 2), BF16),
            pltpu.VMEM((items, slots, hid // 4), BF16),
            pltpu.VMEM((planes, slots, hid // 4), F32),
            pltpu.VMEM((items, slots, hid), BF16),
            pltpu.VMEM((2, cover if pair else width, hid), BF16),
            pltpu.VMEM((planes, slots, width), BF16),
            pltpu.VMEM((planes, slots, width), BF16),
            pltpu.VMEM((planes, 8, lanes), F32),
            pltpu.VMEM((planes, 8, lanes), F32),
            pltpu.VMEM((SLICES, tok_dev, width), BF16),
            pltpu.VMEM((SLICES, 8, tok_dev), F32),
            pltpu.VMEM((SLICES, 8, tok_dev), F32),
            pltpu.VMEM((2, peer, slots, cover), BF16),
            pltpu.VMEM((2 * peer, slots, hid), BF16),
            pltpu.VMEM((planes, slots, SLICES * tok_dev), BF16),
            dma((5,)),
            *pairs,
        ],
        compiler_params=pltpu.CompilerParams(
            collective_id=0, has_side_effects=True, vmem_limit_bytes=56 * 1024 * 1024
        ),
        cost_estimate=pl.CostEstimate(
            flops=12 * planes * slots * width * hid, bytes_accessed=8 * 1024 * 1024, transcendentals=0
        ),
    )(tokens, cotangent, gates.reshape(1, tok_dev), routes.reshape(1, tok_dev), w_up, w_down_t)
    grad_up = sum(up_sums[d].astype(F32) for d in range(sums))
    grad_down_t = sum(down_sums[d].astype(F32) for d in range(sums))
    return grad_tokens, gate_sums.reshape(tok_dev, top_count), grad_up, grad_down_t


def solution(mesh):
    split = P(("rep", "exp"), None)
    weight_split = P(("exp", "rep"), None)
    return jax.shard_map(
        shards,
        mesh=mesh,
        in_specs=(split, split, split, split, weight_split, weight_split),
        out_specs=(split, split, weight_split, weight_split),
        check_vma=False,
    )
```

```python
import functools

import jax
import jax.numpy as jnp
from jax import lax
from jax.experimental import pallas as pl
from jax.experimental.pallas import tpu as pltpu
from jax.sharding import PartitionSpec as P

SLICES = 4
MESH = pl.DeviceIdType.MESH
F32, BF16 = jnp.float32, jnp.bfloat16


def dot(left, right, dims, precision=None):
    return lax.dot_general(
        left, right, ((dims[:1], dims[1:]), ((), ())), preferred_element_type=F32, precision=precision
    )


def tiles(width, step=256):
    return [(start, min(step, width - start)) for start in range(0, width, step)]


def kernel(
    n_rep, planes, capacity, slots, pair, cover,
    tokens, cot, gates, routes, w_up, w_down,
    grad_tokens, gate_sums, up_sums, down_sums,
    cot_block, out_grad, raw, place, weights, packed, rows, part, first, first_in, second_in,
    act, hidden, terms, dx, dx_in, gate_row, gate_in, back, gate_back, gate_mates,
    rows_peer, hidden_peer, matrix,
    local_sem, raw_send, raw_recv, place_send, place_recv, weight_send, weight_recv,
    plane_send, plane_recv, a_send, a_recv, b_send, b_recv, c_send, c_recv, d_send, d_recv,
    dx_send, dx_recv, gate_send, gate_recv, term_send, term_recv, back_send, back_recv,
    mate_send, mate_recv, y_send, y_recv, h_send, h_recv, f_send, f_recv, g_send, g_recv,
):
    rep, me = lax.axis_index("rep"), lax.axis_index("exp")
    plane, q = me // SLICES, me % SLICES
    low, high = q % 2, q // 2
    tok_dev, width = raw.shape[2], raw.shape[3]
    own_rows, hid = w_up.shape
    half, quarter = hid // 2, hid // 4
    items = 2 * planes
    parts = tiles(width, 512)
    last_slot = items - 1

    def mate(distance):
        return (rep, plane * SLICES + (q + distance) % SLICES)

    def ahead(distance):
        return (rep, (plane + distance) % planes * SLICES + q)

    def behind(distance):
        return (rep, (plane + planes - distance) % planes * SLICES + q)

    def replica(distance):
        return ((rep + distance) % n_rep, me)

    near = (rep, plane * SLICES + high * 2 + 1 - low)
    far = (rep, plane * SLICES + (1 - high) * 2 + low)

    def copy(source, target, send_sem, recv_sem, device):
        return pltpu.make_async_remote_copy(
            src_ref=source, dst_ref=target, send_sem=send_sem, recv_sem=recv_sem,
            device_id=device, device_id_type=MESH,
        )

    def feature_block(index):
        return pl.ds(pl.multiple_of(index * width, 128), width)

    def weight_rows(index):
        return pl.ds(pl.multiple_of(index * own_rows, 16), own_rows)

    def feature_part(index, p):
        start, size = parts[p]
        return pl.ds(pl.multiple_of(index * width + start, 128), size)

    def inner(p):
        start, size = parts[p]
        return slice(start, start + size)

    def raw_copy(a, j, p):
        source = (tokens, out_grad)[a]
        return copy(
            source.at[:, feature_part((q + j) % SLICES, p)], raw.at[a, q, :, inner(p)],
            raw_send.at[a, p, j], raw_recv.at[a, p, j], mate(j),
        )

    def place_copy(j):
        return copy(place.at[q], place.at[q], place_send.at[j], place_recv.at[j], mate(j))

    def weight_copy(a, d):
        source = (w_up, w_down)[a]
        return copy(
            source, weights.at[a, weight_rows(rep)],
            weight_send.at[a, d], weight_recv.at[a, d], replica(d),
        )

    def plane_copy(a, k, p):
        return copy(
            packed.at[a, k, :, inner(p)], rows.at[a, k, :, inner(p)],
            plane_send.at[a, p, k], plane_recv.at[a, p, k], ahead(k),
        )

    def a_copy(s):
        other = pl.ds(pl.multiple_of((1 - low) * half, 128), half)
        return copy(part.at[s, :, other], first_in.at[s], a_send.at[s], a_recv.at[s], near)

    def b_copy(s):
        other = pl.ds(pl.multiple_of((1 - high) * quarter, 128), quarter)
        return copy(first.at[s, :, other], second_in.at[s], b_send.at[s], b_recv.at[s], far)

    own_quarter = pl.ds(pl.multiple_of(low * half + high * quarter, 128), quarter)
    own_half = pl.ds(pl.multiple_of(low * half, 128), half)

    def c_copy(s):
        block = hidden.at[s, :, own_quarter]
        return copy(block, block, c_send.at[s], c_recv.at[s], far)

    def d_copy(s):
        block = hidden.at[s, :, own_half]
        return copy(block, block, d_send.at[s], d_recv.at[s], near)

    def dx_copy(k, p):
        return copy(
            dx.at[k, :, inner(p)], dx_in.at[k, :, inner(p)],
            dx_send.at[p, k], dx_recv.at[p, k], behind(k),
        )

    def cover_start(replica_index):
        return jnp.minimum(replica_index * own_rows // 128 * 128, width - cover)

    def y_copy(a, k):
        block = pl.ds(pl.multiple_of(cover_start((rep + 1) % n_rep), 128), cover)
        return copy(
            rows.at[a, k, :, block], rows_peer.at[a, k], y_send.at[a, k], y_recv.at[a, k], replica(1)
        )

    def h_copy(t):
        return copy(
            hidden.at[t, :, own_quarter], hidden_peer.at[t, :, own_quarter],
            h_send.at[t], h_recv.at[t], replica(1),
        )

    def f_copy(t):
        block = hidden_peer.at[t, :, own_quarter]
        return copy(block, block, f_send.at[t], f_recv.at[t], far)

    def g_copy(t):
        block = hidden_peer.at[t, :, own_half]
        return copy(block, block, g_send.at[t], g_recv.at[t], near)

    def gate_copy(k):
        return copy(gate_row.at[k], gate_in.at[k], gate_send.at[k], gate_recv.at[k], behind(k))

    def term_copy(a, d):
        return copy(
            terms.at[a, weight_rows((rep + d) % n_rep)], (up_sums, down_sums)[a].at[d],
            term_send.at[a, d], term_recv.at[a, d], replica(d),
        )

    def back_copy(j, p):
        return copy(
            back.at[(q + j) % SLICES, :, inner(p)], grad_tokens.at[:, feature_part(q, p)],
            back_send.at[p, j], back_recv.at[p, j], mate(j),
        )

    def mate_copy(j):
        return copy(gate_back.at[(q + j) % SLICES], gate_mates.at[j], mate_send.at[j], mate_recv.at[j], mate(j))

    def term_local(a):
        kept = weight_rows(rep)
        if pair:
            kept = pl.ds(pl.multiple_of(rep * own_rows - cover_start(rep), 16), own_rows)
        return pltpu.make_async_copy(
            terms.at[a, kept], (up_sums, down_sums)[a].at[0], local_sem.at[a]
        )

    cot_local = pltpu.make_async_copy(cot, cot_block, local_sem.at[4])
    cot_local.start()
    barrier = pltpu.get_barrier_semaphore()
    peers = [mate(j) for j in range(1, SLICES)] + [replica(d) for d in range(1, n_rep)]
    for device in peers:
        pl.semaphore_signal(barrier, inc=1, device_id=device, device_id_type=MESH)

    @pl.loop(1, planes)
    def _(k):
        pl.semaphore_signal(barrier, inc=1, device_id=ahead(k), device_id_type=MESH)

    pl.semaphore_wait(barrier, len(peers) + planes - 1)

    for j in range(1, SLICES):
        raw_copy(0, j, 0).start()
    for d in range(1, n_rep):
        weight_copy(0, d).start()
    local = [
        pltpu.make_async_copy(tokens.at[:, feature_block(q)], raw.at[0, q], local_sem.at[0]),
        pltpu.make_async_copy(w_up, weights.at[0, weight_rows(rep)], local_sem.at[1]),
        pltpu.make_async_copy(w_down, weights.at[1, weight_rows(rep)], local_sem.at[2]),
    ]
    for c in local:
        c.start()

    route = routes[...]
    count = max(8, planes)
    onehot = (lax.broadcasted_iota(jnp.int32, (count, tok_dev), 0) == route).astype(F32)
    before = (
        lax.broadcasted_iota(jnp.int32, (tok_dev, tok_dev), 0)
        < lax.broadcasted_iota(jnp.int32, (tok_dev, tok_dev), 1)
    ).astype(F32)
    slot = jnp.sum(onehot * dot(onehot, before, (1, 0)), axis=0, keepdims=True)
    position = (route * slots + q * capacity).astype(F32) + slot
    place[q] = jnp.broadcast_to(position, (8, tok_dev))
    for j in range(1, SLICES):
        place_copy(j).start()
    for p in range(1, len(parts)):
        for j in range(1, SLICES):
            raw_copy(0, j, p).start()

    square = lax.broadcasted_iota(jnp.int32, (tok_dev, tok_dev), 0) == lax.broadcasted_iota(
        jnp.int32, (tok_dev, tok_dev), 1
    )
    gate = jnp.sum(jnp.where(square, gates[...], 0.0), axis=1, keepdims=True)
    cot_local.wait()
    for m in range(SLICES):
        block = slice(m * width, (m + 1) * width)
        out_grad[:, block] = (gate * cot_block[:, block].astype(F32)).astype(BF16)
    local_grad = pltpu.make_async_copy(
        out_grad.at[:, feature_block(q)], raw.at[1, q], local_sem.at[3]
    )
    local_grad.start()
    gate_row[...] = jnp.zeros_like(gate_row)

    for j in range(1, SLICES):
        place_copy(j).wait_recv()
    places = jnp.concatenate([place[m, 0:1, :] for m in range(SLICES)], axis=1)

    @pl.loop(0, planes)
    def _(k):
        number = lax.broadcasted_iota(jnp.int32, (slots, SLICES * tok_dev), 0)
        number = (number + (plane + k) % planes * slots).astype(F32)
        matrix[k] = jnp.where(number == places, 1.0, 0.0).astype(BF16)

    def pack(a, k, p, target):
        begin, length = parts[p]
        for start, size in tiles(length):
            block = slice(begin + start, begin + start + size)
            source = raw[a, :, :, block].reshape(SLICES * tok_dev, size)
            target[a, k, :, block] = dot(matrix[k], source, (1, 0)).astype(BF16)

    for a in range(2):
        (local[0], local_grad)[a].wait()
        for p in range(len(parts)):
            for j in range(1, SLICES):
                landed = raw.at[a, (q + SLICES - j) % SLICES, :, inner(p)]
                copy(
                    landed, landed, raw_send.at[a, p, j], raw_recv.at[a, p, j], mate(j)
                ).wait_recv()
            if a == 0:
                for j in range(1, SLICES):
                    raw_copy(1, j, p).start()

            @pl.loop(1, planes)
            def _(k):
                pack(a, k, p, packed)
                plane_copy(a, k, p).start()

            pack(a, 0, p, rows)
        if pair:
            y_copy(a, 0).start()
    local[1].wait()
    local[2].wait()

    def dx_product(k, p, target):
        left = hidden[planes + k]
        begin, length = parts[p]
        for start, size in tiles(length):
            block = slice(begin + start, begin + start + size)
            target[k, :, block] = dot(left, weights[0, block, :], (1, 1)).astype(BF16)

    def split(value):
        upper = value.astype(BF16)
        return upper, (value - upper.astype(F32)).astype(BF16)

    def weight_term(a):
        right = hidden[(1 - a) * planes : (2 - a) * planes].reshape(planes * slots, hid)
        for start, size in tiles(width, 512):
            left = rows[a, :, :, start : start + size].reshape(planes * slots, size)
            terms[a, start : start + size, :] = dot(left, right, (0, 0)).astype(BF16)
        for d in range(1, n_rep):
            term_copy(a, d).start()
        term_local(a).start()

    def pair_term(a):
        @pl.loop((1 - a) * planes, (2 - a) * planes)
        def _(t):
            landed = hidden_peer.at[t, :, pl.ds(pl.multiple_of((1 - low) * half, 128), half)]
            copy(landed, landed, g_send.at[t], g_recv.at[t], near).wait_recv()

        @pl.loop(0, planes)
        def _(k):
            landed = rows_peer.at[a, k]
            copy(landed, landed, y_send.at[a, k], y_recv.at[a, k], replica(1)).wait_recv()

        count = planes * slots
        mine = pl.ds(pl.multiple_of(cover_start(rep), 128), cover)
        some = slice((1 - a) * planes, (2 - a) * planes)
        total = dot(
            rows[a, :, :, mine].reshape(count, cover), hidden[some].reshape(count, hid), (0, 0)
        )
        total += dot(
            rows_peer[a].reshape(count, cover), hidden_peer[some].reshape(count, hid), (0, 0)
        )
        terms[a] = total.astype(BF16)
        term_local(a).start()

    @pl.loop(0, last_slot + (7 if pair else 6))
    def _(s):
        def stage(lag):
            return s - lag, (s >= lag) & (s <= last_slot + lag)

        e_item, e_here = stage(4)

        @pl.when(e_here)
        def _():
            t = e_item
            landed = hidden.at[t, :, pl.ds(pl.multiple_of((1 - low) * half, 128), half)]
            copy(landed, landed, d_send.at[t], d_recv.at[t], near).wait_recv()

            @pl.when(t >= planes)
            def _():
                k = t - planes
                @pl.when(k == 0)
                def _():
                    for p in range(len(parts)):
                        dx_product(0, p, dx_in)

                @pl.when(k > 0)
                def _():
                    dx_product(k, 0, dx)
                    dx_copy(k, 0).start()
                    gate_copy(k).start()

        d_item, d_here = stage(3)

        @pl.when(d_here)
        def _():
            t = d_item
            landed = hidden.at[
                t, :, pl.ds(pl.multiple_of(low * half + (1 - high) * quarter, 128), quarter)
            ]
            copy(landed, landed, c_send.at[t], c_recv.at[t], far).wait_recv()
            d_copy(t).start()

        c_item, c_here = stage(2)

        @pl.when(c_here)
        def _():
            t = c_item
            b_copy(t).wait_recv()
            mine = pl.ds(pl.multiple_of(high * quarter, 128), quarter)
            total = first[t, :, mine].astype(F32) + second_in[t].astype(F32)

            @pl.when(t < planes)
            def _():
                act[t] = total
                hidden[t, :, own_quarter] = (total * jax.nn.sigmoid(total)).astype(BF16)

            @pl.when(t >= planes)
            def _():
                k = t - planes
                value = act[k]
                gating = jax.nn.sigmoid(value)
                hidden[t, :, own_quarter] = (
                    total * gating * (1.0 + value * (1.0 - gating))
                ).astype(BF16)
                upper, lower = split(total * (value * gating))
                ones = jnp.ones((16, quarter), BF16)
                sums = dot(ones, upper, (1, 1)) + dot(ones, lower, (1, 1))
                gate_row[k, :, 0:slots] = sums[0:8]

            c_copy(t).start()
            if pair:
                h_copy(t).start()

        b_item, b_here = stage(1)

        @pl.when(b_here)
        def _():
            t = b_item
            a_copy(t).wait_recv()
            first[t] = (part[t, :, own_half].astype(F32) + first_in[t].astype(F32)).astype(BF16)
            b_copy(t).start()

        i, here = stage(0)

        @pl.when(here)
        def _():
            a, k = i // planes, i % planes

            @pl.when(k == 0)
            def _():
                for d in range(1, n_rep):
                    landed = weights.at[a, weight_rows((rep + n_rep - d) % n_rep)]
                    copy(
                        landed, landed, weight_send.at[a, d], weight_recv.at[a, d], replica(d)
                    ).wait_recv()

                @pl.when(a == 0)
                def _():
                    for d in range(1, n_rep):
                        weight_copy(1, d).start()

            @pl.when(k > 0)
            def _():
                for p in range(len(parts)):
                    plane_copy(a, k, p).wait_recv()
                if pair:
                    y_copy(a, k).start()

            left = rows[a, k]
            for start, size in tiles(hid):
                part[i, :, start : start + size] = dot(
                    left, weights[a, :, start : start + size], (1, 0)
                ).astype(BF16)
            a_copy(i).start()

        @pl.when(s == last_slot + 5)
        def _():
            for p in range(1, len(parts)):
                @pl.loop(1, planes)
                def _(k):
                    dx_product(k, p, dx)
                    dx_copy(k, p).start()

        if pair:
            f_item, f_here = stage(5)

            @pl.when(f_here)
            def _():
                h_copy(f_item).wait_recv()
                f_copy(f_item).start()

            g_item, g_here = stage(6)

            @pl.when(g_here)
            def _():
                t = g_item
                landed = hidden_peer.at[
                    t, :, pl.ds(pl.multiple_of(low * half + (1 - high) * quarter, 128), quarter)
                ]
                copy(landed, landed, f_send.at[t], f_recv.at[t], far).wait_recv()
                g_copy(t).start()

            @pl.when(s == last_slot + 6)
            def _():
                pair_term(1)
        else:
            @pl.when(s == last_slot + 3)
            def _():
                weight_term(1)

    if not pair:
        weight_term(0)

    @pl.loop(1, planes)
    def _(k):
        gate_copy(k).wait_recv()

    for p in range(len(parts)):
        @pl.loop(1, planes)
        def _(k):
            dx_copy(k, p).wait_recv()

        every = matrix[...].reshape(planes * slots, SLICES * tok_dev)
        landed = dx_in[:, :, inner(p)].reshape(planes * slots, parts[p][1])
        token_rows = dot(every, landed, (0, 0)).astype(BF16)
        back[:, :, inner(p)] = token_rows.reshape(SLICES, tok_dev, parts[p][1])
        for j in (2, 1, 3):
            back_copy(j, p).start()
        if p == 0:
            sums = jnp.zeros((8, SLICES * tok_dev), F32)
            for k in range(planes):
                upper, lower = split((gate_row if k == 0 else gate_in)[k, :, 0:slots])
                both = dot(jnp.concatenate([upper, lower], axis=0), matrix[k], (1, 0))
                sums += both[0:8] + both[8:16]
            for m in range(SLICES):
                gate_back[m] = sums[:, m * tok_dev : (m + 1) * tok_dev]
            for j in range(1, SLICES):
                mate_copy(j).start()
            if pair:
                pair_term(0)
    last = pltpu.make_async_copy(
        back.at[q], grad_tokens.at[:, feature_block(q)], local_sem.at[2]
    )
    last.start()
    total = gate_back[q]
    for j in range(1, SLICES):
        mate_copy(j).wait_recv()
        total += gate_mates[j]
    gate_sums[...] = total[0:1] / gates[...]
    last.wait()
    for p in range(len(parts)):
        for j in range(1, SLICES):
            landed = grad_tokens.at[:, feature_part((q + SLICES - j) % SLICES, p)]
            copy(landed, landed, back_send.at[p, j], back_recv.at[p, j], mate(j)).wait_recv()
            back_copy(j, p).wait_send()
    for a in range(2):
        term_local(a).wait()
        for d in range(1, n_rep):
            if not pair:
                term_copy(a, d).wait_recv()
                term_copy(a, d).wait_send()
            weight_copy(a, d).wait_send()
        for j in range(1, SLICES):
            for p in range(len(parts)):
                raw_copy(a, j, p).wait_send()

        @pl.loop(1, planes)
        def _(k):
            for p in range(len(parts)):
                plane_copy(a, k, p).wait_send()

    for j in range(1, SLICES):
        place_copy(j).wait_send()
        mate_copy(j).wait_send()

    @pl.loop(1, planes)
    def _(k):
        for p in range(len(parts)):
            dx_copy(k, p).wait_send()
        gate_copy(k).wait_send()

    @pl.loop(0, items)
    def _(s):
        a_copy(s).wait_send()
        b_copy(s).wait_send()
        c_copy(s).wait_send()
        d_copy(s).wait_send()
        if pair:
            h_copy(s).wait_send()
            f_copy(s).wait_send()
            g_copy(s).wait_send()
            y_copy(s // planes, s % planes).wait_send()


def shards(tokens, cotangent, gates, routes, w_up, w_down_t):
    tok_dev, top_count = routes.shape
    model_width = tokens.shape[1]
    width = model_width // SLICES
    n_rep, n_exp = lax.axis_size("rep"), lax.axis_size("exp")
    planes = n_exp // SLICES
    capacity = min(tok_dev, max(2, 9 * tok_dev * top_count // (8 * planes)))
    slots = -(-SLICES * capacity // 16) * 16
    lanes = -(-slots // 128) * 128
    own_rows, hid = w_up.shape
    items = 2 * planes
    pair = n_rep == 2
    cover = max(
        -(-(r + 1) * own_rows // 128) * 128 - r * own_rows // 128 * 128 for r in range(n_rep)
    )
    sums = 1 if pair else n_rep
    peer = planes if pair else 1
    n_parts = len(tiles(width, 512))
    dma = pltpu.SemaphoreType.DMA
    vmem = pl.BlockSpec(memory_space=pltpu.VMEM)
    hbm = pl.BlockSpec(memory_space=pl.ANY)
    pairs = []
    for shape in (
        (2, n_parts, SLICES), (SLICES,), (2, n_rep), (2, n_parts, planes), (items,), (items,), (items,), (items,),
        (n_parts, planes), (planes,), (2, n_rep), (n_parts, SLICES), (SLICES,),
        (2, planes), (items,), (items,), (items,),
    ):
        pairs += [dma(shape), dma(shape)]
    grad_tokens, gate_sums, up_sums, down_sums = pl.pallas_call(
        functools.partial(kernel, n_rep, planes, capacity, slots, pair, cover),
        out_shape=(
            jax.ShapeDtypeStruct((tok_dev, model_width), BF16),
            jax.ShapeDtypeStruct((1, tok_dev), F32),
            jax.ShapeDtypeStruct((sums, own_rows, hid), BF16),
            jax.ShapeDtypeStruct((sums, own_rows, hid), BF16),
        ),
        in_specs=[hbm, hbm, vmem, vmem, hbm, hbm],
        out_specs=(hbm, vmem, hbm, hbm),
        scratch_shapes=[
            pltpu.VMEM((tok_dev, model_width), BF16),
            pltpu.VMEM((tok_dev, model_width), BF16),
            pltpu.VMEM((2, SLICES, tok_dev, width), BF16),
            pltpu.VMEM((SLICES, 8, tok_dev), F32),
            pltpu.VMEM((2, width, hid), BF16),
            pltpu.VMEM((2, planes, slots, width), BF16),
            pltpu.VMEM((2, planes, slots, width), BF16),
            pltpu.VMEM((items, slots, hid), BF16),
            pltpu.VMEM((items, slots, hid // 2), BF16),
            pltpu.VMEM((items, slots, hid // 2), BF16),
            pltpu.VMEM((items, slots, hid // 4), BF16),
            pltpu.VMEM((planes, slots, hid // 4), F32),
            pltpu.VMEM((items, slots, hid), BF16),
            pltpu.VMEM((2, cover if pair else width, hid), BF16),
            pltpu.VMEM((planes, slots, width), BF16),
            pltpu.VMEM((planes, slots, width), BF16),
            pltpu.VMEM((planes, 8, lanes), F32),
            pltpu.VMEM((planes, 8, lanes), F32),
            pltpu.VMEM((SLICES, tok_dev, width), BF16),
            pltpu.VMEM((SLICES, 8, tok_dev), F32),
            pltpu.VMEM((SLICES, 8, tok_dev), F32),
            pltpu.VMEM((2, peer, slots, cover), BF16),
            pltpu.VMEM((2 * peer, slots, hid), BF16),
            pltpu.VMEM((planes, slots, SLICES * tok_dev), BF16),
            dma((5,)),
            *pairs,
        ],
        compiler_params=pltpu.CompilerParams(
            collective_id=0, has_side_effects=True, vmem_limit_bytes=56 * 1024 * 1024
        ),
        cost_estimate=pl.CostEstimate(
            flops=12 * planes * slots * width * hid, bytes_accessed=8 * 1024 * 1024, transcendentals=0
        ),
    )(tokens, cotangent, gates.reshape(1, tok_dev), routes.reshape(1, tok_dev), w_up, w_down_t)
    grad_up = sum(up_sums[d].astype(F32) for d in range(sums))
    grad_down_t = sum(down_sums[d].astype(F32) for d in range(sums))
    return grad_tokens, gate_sums.reshape(tok_dev, top_count), grad_up, grad_down_t


def solution(mesh):
    split = P(("rep", "exp"), None)
    weight_split = P(("exp", "rep"), None)
    return jax.shard_map(
        shards,
        mesh=mesh,
        in_specs=(split, split, split, split, weight_split, weight_split),
        out_specs=(split, split, weight_split, weight_split),
        check_vma=False,
    )
```
